32 devices in a mesh: seg: 8 (over y, x, core), gx: 4 (over z).
Axes of the slice: x: 2, y: 2, z: 4, core: 2. Of those that a mesh axis runs over, the one named last changes fastest.
Arguments:
- adjoint_in: float32 [8, 5, 64, 32, 512], P('seg', None, 'gx'), may hold values from -6 to 6
- sensor: float32 [8, 64, 32, 512], P('seg', 'gx'), may hold values from 0.06 to 0.15
- filter_matrix: float32 [512, 512], replicated
- coupling: float32 [5, 5], replicated
Outputs:
- adjoint_out: float32 [8, 5, 64, 32, 512], P('seg', None, 'gx')
The draws below stay inside these ranges and needn't reach their ends.
All inputs are finite; a program needn't handle non-finite values.
Results may differ from the reference program's by a relative error of at most 0.00017.
Values sent between devices are 32-bit elements; how exact they have to be, the bound alone decides.
No kernel may reach another device: no remote copies, remote signals or barrier semaphores. Data moves between devices by JAX's collectives and lax.ppermute only.
A program may use at most 64 MiB of HBM per device.

```python
import math
import jax
import jax.numpy as jnp
from jax import lax

FIELDS = 5
NR = 512
STEPS = 3
CX = 16
NTH = 32
NSEG = 8
NX = 64


def draw_adjoint_in(key, part):
    level_key = jax.random.fold_in(key, 11)
    noise_key = jax.random.fold_in(key, 23)
    blocks = NX // CX
    levels = jnp.exp(jax.random.uniform(level_key, (NSEG, 1, blocks, 1, 1, 1), jnp.float32, -3.0, 1.0))
    shape = (NSEG, FIELDS, blocks, CX, NTH, NR)
    noise = jax.random.truncated_normal(noise_key, -4.0, 4.0, shape, jnp.float32)
    values = jnp.clip(noise * levels, -6.0, 6.0)
    return values.reshape(NSEG, FIELDS, NX, NTH, NR)


def draw_filter_matrix(key, part):
    noise = jax.random.truncated_normal(key, -4.0, 4.0, (NR, NR), jnp.float32)
    return 0.6 * jnp.eye(NR, dtype=jnp.float32) + noise * (0.5 / math.sqrt(NR))


def draw_coupling(key, part):
    noise = jax.random.truncated_normal(key, -4.0, 4.0, (FIELDS, FIELDS), jnp.float32)
    return jnp.eye(FIELDS, dtype=jnp.float32) + 0.25 * noise


def shard_levels(own_key, shape, cuts, smallest, high):
    def one(dim, parts):
        draws = jax.random.uniform(jax.random.fold_in(jax.random.fold_in(own_key, 6), dim), (parts,), jnp.float32, smallest / len(cuts), high / len(cuts))
        return jnp.repeat(jnp.exp(draws), shape[dim] // parts).reshape((-1,) + (1,) * (len(shape) - dim - 1))

    level = one(*cuts[0])
    for cut in cuts[1:]:
        level = level * one(*cut)
    return level


def setup_inputs(seed: int = 0) -> dict:
    key_of = jax.random.split(jax.random.key(seed), 5)
    adjoint_in = draw_adjoint_in(jax.random.fold_in(key_of[4], 71), 0)
    sensor = jnp.clip(jnp.exp(math.log(0.15) - 0.9162908 * jax.random.uniform(key_of[1], (NSEG, NX, NTH, NR), jnp.float32) ** shard_levels(key_of[1], (NSEG, NX, NTH, NR), ((0, 8), (1, 4)), -0.2, 0.2)), 0.06, 0.15)
    filter_matrix = draw_filter_matrix(jax.random.fold_in(key_of[4], 71), 0)
    coupling = draw_coupling(jax.random.fold_in(key_of[4], 71), 0)
    return dict(adjoint_in=adjoint_in, sensor=sensor, filter_matrix=filter_matrix, coupling=coupling)


def filter_rows(state, filter_matrix):
    dims_shape = state.shape
    flat = state.reshape(-1, dims_shape[-1])
    result = jnp.dot(flat, filter_matrix, precision=lax.Precision.HIGHEST, preferred_element_type=jnp.float32)
    return result.reshape(dims_shape)


def mix_fields(filtered, coupling):
    return jnp.einsum("gf,gxyr->fxyr", coupling, filtered, precision=lax.Precision.HIGHEST)


def laplace(padded):
    middle = padded[:, 1:-1]
    widened = jnp.pad(middle, ((0, 0), (0, 0), (1, 1), (1, 1)))
    laplacian = padded[:, 2:] + padded[:, :-2]
    laplacian = laplacian + widened[:, :, 2:, 1:-1] + widened[:, :, :-2, 1:-1]
    laplacian = laplacian + widened[:, :, 1:-1, 2:] + widened[:, :, 1:-1, :-2]
    return laplacian - 6.0 * middle


def reference(adjoint_in, sensor, filter_matrix, coupling):
    incoming = jnp.roll(adjoint_in, -1, axis=0)

    def propagate(inputs_pair):
        state, sensor_cell = inputs_pair
        for step in range(STEPS):
            filtered = filter_rows(state, filter_matrix)
            mixed = mix_fields(filtered, coupling)
            padded = jnp.pad(mixed, ((0, 0), (1, 1), (0, 0), (0, 0)))
            state = filtered + sensor_cell[None] * laplace(padded)
        return state

    carried = lax.map(propagate, (incoming, sensor))
    return carried - adjoint_in
```

```python
import functools

import jax
import jax.numpy as jnp
from jax import lax
from jax.experimental import pallas as pl
from jax.experimental.pallas import tpu as pltpu
from jax.sharding import PartitionSpec as P

STEPS = 3
LANES = 128
PAD = 8
ROWS = 16
GROUPS = (1, 1, 1, 2, 2)
VMEM_LIMIT = 56 * 1024 * 1024


class Stage:
    def __init__(self, start, stop, half):
        self.start, self.stop, self.half = start, stop, half
        self.first, self.last = start == -STEPS, stop == half
        self.todo = {}
        for level in range(1, STEPS + 2):
            lag = level - 1
            low = start + lag if self.first else start - lag
            self.todo[level] = (low, stop if self.last else stop - lag)
        self.base = {}
        self.slots = {}
        for level in range(1, STEPS + 1):
            low, high = self.todo[level]
            self.base[level] = low if self.first else low - 2
            self.slots[level] = high - self.base[level]
        self.sensor_low = self.todo[STEPS + 1][0] if not self.first else self.todo[2][0]
        self.sensor_high = self.todo[2][1]


def stage_kernel(stage, fields, planes, groups, *refs):
    refs = list(refs)

    def take(count):
        got = refs[:count]
        del refs[:count]
        return got

    (coupling, weights_in, own_in, sensor_in) = take(4)
    chunks_in = take(len(groups))
    halos_in = take(2 * STEPS) if stage.first else []
    sensor_halo_in = take(2) if stage.first else []
    carries_in = [] if stage.first else take(STEPS)
    if not stage.first:
        take(1)
    (out,) = take(1)
    carries_out = [] if stage.last else take(STEPS)
    (weights, own, sensor, raw) = take(4)
    filtered = dict(zip(range(1, STEPS + 1), take(STEPS)))
    highs = take(2)
    lows = take(2)
    (sems,) = take(1)

    sides = 2 * fields
    nth = raw.shape[-2]
    blocks = raw.shape[-1] // LANES
    used = [0]

    def copy(source, target):
        made = pltpu.make_async_copy(source, target, sems.at[used[0]])
        used[0] += 1
        made.start()
        return made

    waits = {level: [] for level in range(1, STEPS + 2)}
    waits[1].append(copy(weights_in, weights))
    low = stage.todo[1][0]
    if stage.first:
        for h in range(STEPS):
            for s in range(2):
                waits[1].append(copy(halos_in[2 * h + s], raw.at[-1 - h - low, s]))
    depth = max(low, 0)
    for ref, count in zip(chunks_in, groups):
        waits[1].append(copy(ref, raw.at[pl.ds(depth - low, count)]))
        depth += count
    if not stage.first:
        for level in range(1, STEPS + 1):
            waits[level + 1].append(
                copy(carries_in[level - 1], filtered[level].at[pl.ds(0, 2 * sides)])
            )
    for q in range(stage.sensor_high - 1, stage.sensor_low - 1, -1):
        for s in range(2):
            target = sensor.at[q - stage.sensor_low, s]
            if q < 0:
                source = sensor_halo_in[s].at[-1 - q]
            else:
                source = sensor_in.at[0, planes - 1 - q if s else q]
            waits[2].append(copy(source, target))
    out_low, out_high = stage.todo[STEPS + 1]
    for q in range(out_low, out_high):
        for s in range(2):
            plane = planes - 1 - q if s else q
            waits[STEPS + 1].append(copy(own_in.at[0, :, plane], own.at[q - out_low, s]))

    blank = jnp.zeros((PAD, LANES), jnp.float32)
    for level in range(1, STEPS + 1):
        skip = 0 if stage.first else 2 * sides
        ref = filtered[level]

        def clear(i, ref=ref):
            for b in range(blocks):
                ref[i, b, 0:PAD] = blank
                ref[i, b, PAD + nth : 2 * PAD + nth] = blank

        pl.loop(skip, ref.shape[0])(clear)

    lane = lax.broadcasted_iota(jnp.int32, (ROWS, LANES), 1)
    at_start = lane == 0
    at_end = lane == LANES - 1

    def put(value, place, row, b):
        high = value.astype(jnp.bfloat16)
        highs[place][row : row + ROWS, b * LANES : (b + 1) * LANES] = high
        low_part = value - high.astype(jnp.float32)
        lows[place][row : row + ROWS, b * LANES : (b + 1) * LANES] = low_part.astype(jnp.bfloat16)

    def split_raw(q, place):
        slot = q - stage.todo[1][0]
        for s in range(2):
            for f in range(fields):
                for t in range(0, nth, ROWS):
                    for b in range(blocks):
                        value = raw[slot, s, f, t : t + ROWS, b * LANES : (b + 1) * LANES]
                        put(value, place, (s * fields + f) * nth + t, b)

    def advance(level, q, place):
        ref = filtered[level - 1]
        slot = q - stage.base[level - 1]
        inner = not isinstance(q, int) or q < stage.half - 1
        for s in range(2):
            here = slot * sides + s * fields
            before = here - sides
            after = here + sides if inner else slot * sides + (1 - s) * fields
            for t in range(0, nth, ROWS):
                laps = []
                for f in range(fields):
                    middle = [ref[here + f, b, PAD + t : PAD + t + ROWS] for b in range(blocks)]
                    up = [pltpu.roll(v, 1, 1) for v in middle]
                    down = [pltpu.roll(v, LANES - 1, 1) for v in middle]
                    row = []
                    for b in range(blocks):
                        lap = ref[before + f, b, PAD + t : PAD + t + ROWS]
                        lap = lap + ref[after + f, b, PAD + t : PAD + t + ROWS]
                        lap = lap + ref[here + f, b, PAD + t - 1 : PAD + t - 1 + ROWS]
                        lap = lap + ref[here + f, b, PAD + t + 1 : PAD + t + 1 + ROWS]
                        lap = lap + jnp.where(at_start, up[b - 1] if b else 0.0, up[b])
                        lap = lap + jnp.where(
                            at_end, down[b + 1] if b + 1 < blocks else 0.0, down[b]
                        )
                        row.append(lap - 6.0 * middle[b])
                    laps.append(row)
                for b in range(blocks):
                    sens = sensor[q - stage.sensor_low, s, t : t + ROWS, b * LANES : (b + 1) * LANES]
                    for f in range(fields):
                        mixed = coupling[0, f] * laps[0][b]
                        for g in range(1, fields):
                            mixed = mixed + coupling[g, f] * laps[g][b]
                        value = ref[here + f, b, PAD + t : PAD + t + ROWS] + sens * mixed
                        if level == STEPS + 1:
                            at = (q - out_low, s, f, slice(t, t + ROWS), slice(b * LANES, (b + 1) * LANES))
                            own[at] = value - own[at]
                        else:
                            put(value, place, (s * fields + f) * nth + t, b)

    def project(level, q, place):
        ref = filtered[level]
        slot = q - stage.base[level]
        high = highs[place][...]
        left = jnp.concatenate([high, lows[place][...], high], axis=1)
        width = 2 * LANES
        for n in range(0, blocks * LANES, width):
            result = jnp.dot(left, weights[:, n : n + width], preferred_element_type=jnp.float32)
            for i in range(sides):
                for b in range(width // LANES):
                    ref[slot * sides + i, n // LANES + b, PAD : PAD + nth] = result[
                        i * nth : (i + 1) * nth, b * LANES : (b + 1) * LANES
                    ]

    def work(level, q, place):
        if level == 1:
            split_raw(q, place)
        else:
            advance(level, q, place)

    def send_out(q):
        sent = []
        for s in range(2):
            plane = planes - 1 - q if s else q
            sent.append(copy(own.at[q - out_low, s], out.at[0, :, plane]))
        return sent

    def ready(level):
        for made in waits[level]:
            made.wait()

    finish = []
    if stage.last:
        held = None
        for level in range(1, STEPS + 2):
            ready(level)
            for q in range(*stage.todo[level]):
                place = 0 if held is None else 1 - held[2]
                if held is not None:
                    project(*held)
                work(level, q, place)
                held = (level, q, place) if level <= STEPS else None
                if level == STEPS + 1:
                    finish += send_out(q)
    else:
        for level in range(1, STEPS + 2):
            ready(level)

            def step(q, level=level):
                work(level, q, 0)
                if level <= STEPS:
                    project(level, q, 0)

            pl.loop(*stage.todo[level])(step)
            if level <= STEPS:
                ref = filtered[level]
                finish.append(
                    copy(ref.at[pl.ds(ref.shape[0] - 2 * sides, 2 * sides)], carries_out[level - 1])
                )
        for q in range(out_low, out_high):
            finish += send_out(q)
    for made in finish:
        made.wait()


def run_stage(stage, groups, coupling, weights, own, sensor, chunks, halos, sensor_halos, carries, out):
    fields, planes, nth, nr = own.shape[1:]
    sides = 2 * fields
    blocks = nr // LANES
    held = nth + 2 * PAD
    anywhere = pl.BlockSpec(memory_space=pl.ANY)
    operands = [coupling, weights, own, sensor, *chunks]
    if stage.first:
        operands += [*halos, *sensor_halos]
    else:
        operands += [*carries, out]
    in_specs = [pl.BlockSpec(memory_space=pltpu.SMEM)] + [anywhere] * (len(operands) - 1)
    out_shape = [jax.ShapeDtypeStruct(own.shape, jnp.float32)]
    if not stage.last:
        out_shape += [jax.ShapeDtypeStruct((2 * sides, blocks, held, LANES), jnp.float32)] * STEPS
    low, high = stage.todo[1]
    outs = stage.todo[STEPS + 1][1] - stage.todo[STEPS + 1][0]
    depths = stage.sensor_high - stage.sensor_low
    copies = 1 + len(chunks) + 2 * STEPS + 2 + STEPS * 2 + 2 * depths + 4 * outs
    scratch = [
        pltpu.VMEM(weights.shape, jnp.bfloat16),
        pltpu.VMEM((outs, 2, fields, nth, nr), jnp.float32),
        pltpu.VMEM((depths, 2, nth, nr), jnp.float32),
        pltpu.VMEM((high - low, 2, fields, nth, nr), jnp.float32),
        *[
            pltpu.VMEM((stage.slots[level] * sides, blocks, held, LANES), jnp.float32)
            for level in range(1, STEPS + 1)
        ],
        *[pltpu.VMEM((sides * nth, nr), jnp.bfloat16)] * 4,
        pltpu.SemaphoreType.DMA((copies,)),
    ]
    dots = sum(stage.todo[level][1] - stage.todo[level][0] for level in range(1, STEPS + 1))
    flops = dots * 2 * sides * nth * nr * nr * 3
    return pl.pallas_call(
        functools.partial(stage_kernel, stage, fields, planes, groups),
        out_shape=out_shape,
        in_specs=in_specs,
        out_specs=[anywhere] * len(out_shape),
        scratch_shapes=scratch,
        input_output_aliases={} if stage.first else {len(operands) - 1: 0},
        cost_estimate=pl.CostEstimate(
            flops=flops * 2, bytes_accessed=8 * (high - low) * sides * nth * nr, transcendentals=0
        ),
        compiler_params=pltpu.CompilerParams(vmem_limit_bytes=VMEM_LIMIT),
        name=f"stage_{'first' if stage.first else 'last' if stage.last else 'middle'}",
    )(*operands)


def shards(adjoint_in, sensor, filter_matrix, coupling):
    fields, planes, nth, nr = adjoint_in.shape[1:]
    half = planes // 2
    segs = lax.axis_size("seg")
    slabs = lax.axis_size("gx")
    back = [((i + 1) % segs, i) for i in range(segs)]
    up = [(i, i + 1) for i in range(slabs - 1)]
    down = [(i + 1, i) for i in range(slabs - 1)]

    groups = []
    for count in GROUPS:
        if sum(groups) + count < half:
            groups.append(count)
    groups.append(half - sum(groups))

    own = adjoint_in[0]
    chunks = []
    depth = 0
    for count in groups:
        parts = []
        for q in range(depth, depth + count):
            parts += [own[:, q], own[:, planes - 1 - q]]
        packed = jnp.stack(parts).reshape(count, 2, fields, nth, nr)
        chunks.append(lax.ppermute(packed, "seg", back))
        depth += count

    sensor_halos = [
        lax.ppermute(jnp.flip(sensor[0, planes - (STEPS - 1) :], 0), "gx", up),
        lax.ppermute(sensor[0, : STEPS - 1], "gx", down),
    ]
    halos = []
    for h in range(STEPS):
        halos.append(lax.ppermute(chunks[h][0, 1], "gx", up))
        halos.append(lax.ppermute(chunks[h][0, 0], "gx", down))

    high = lax.reduce_precision(filter_matrix, 8, 7)
    low = filter_matrix - high
    weights = jnp.concatenate([high, high, low], axis=0).astype(jnp.bfloat16)

    cuts = [0, len(groups) - 2, len(groups) - 1, len(groups)]
    carries, out = None, None
    depth = 0
    for low_cut, high_cut in zip(cuts[:-1], cuts[1:]):
        mine = groups[low_cut:high_cut]
        stage = Stage(depth if low_cut else -STEPS, depth + sum(mine), half)
        depth += sum(mine)
        out, *carries = run_stage(
            stage, mine, coupling, weights, adjoint_in, sensor,
            chunks[low_cut:high_cut], halos, sensor_halos, carries, out,
        )
    return out


def solution(mesh):
    in_specs = (P("seg", None, "gx", None, None), P("seg", "gx", None, None), P(), P())
    out_specs = P("seg", None, "gx", None, None)
    return jax.shard_map(shards, mesh=mesh, in_specs=in_specs, out_specs=out_specs, check_vma=False)
```

```python
import functools
import math

import jax
import jax.numpy as jnp
from jax import lax
from jax.experimental import pallas as pl
from jax.experimental.pallas import tpu as pltpu
from jax.sharding import PartitionSpec as P

STEPS = 3
LANES = 128
PAD = 8
ROWS = 16
GROUPS = (1, 1, 1, 2, 2)
VMEM_SPARE = 6 * 1024 * 1024
VMEM_MOST = 60 * 1024 * 1024


class Stage:
    def __init__(self, start, stop, half):
        self.start, self.stop, self.half = start, stop, half
        self.first, self.last = start == -STEPS, stop == half
        self.todo = {}
        for level in range(1, STEPS + 2):
            lag = level - 1
            low = start + lag if self.first else start - lag
            self.todo[level] = (low, stop if self.last else stop - lag)
        self.base = {}
        self.slots = {}
        for level in range(1, STEPS + 1):
            low, high = self.todo[level]
            self.base[level] = low if self.first else low - 2
            self.slots[level] = high - self.base[level]
        self.sensor_low = self.todo[STEPS + 1][0] if not self.first else self.todo[2][0]
        self.sensor_high = self.todo[2][1]


def pack_kernel(plan, *refs):
    sems = refs[-1]
    made = []
    for i, (operand, source, result, target) in enumerate(plan):
        made.append(pltpu.make_async_copy(refs[operand].at[source], refs[result].at[target], sems.at[i]))
        made[-1].start()
    for one in made:
        one.wait()


def stage_kernel(stage, fields, planes, groups, *refs):
    refs = list(refs)

    def take(count):
        got = refs[:count]
        del refs[:count]
        return got

    (coupling, odd_ref, weights_in, own_in, sensor_in) = take(5)
    chunks_in = take(len(groups))
    halos_in = take(2 * STEPS) if stage.first else []
    sensor_halo_in = take(2) if stage.first else []
    carries_in = [] if stage.first else take(STEPS)
    if not stage.first:
        take(1)
    (out,) = take(1)
    carries_out = [] if stage.last else take(STEPS)
    (weights, own, sensor, raw) = take(4)
    filtered = dict(zip(range(1, STEPS + 1), take(STEPS)))
    highs = take(2)
    lows = take(2)
    (sems,) = take(1)

    sides = 2 * fields
    nth = raw.shape[-2]
    blocks = raw.shape[-1] // LANES
    used = [0]

    def copy(source, target):
        made = pltpu.make_async_copy(source, target, sems.at[used[0]])
        used[0] += 1
        made.start()
        return made

    waits = {level: [] for level in range(1, STEPS + 2)}
    low = stage.todo[1][0]
    depth = max(low, 0)
    for ref, count in zip(chunks_in, groups):
        waits[1].append(copy(ref, raw.at[pl.ds(depth - low, count)]))
        depth += count
    waits[1].append(copy(weights_in, weights))
    odd = odd_ref[0]
    if stage.first:
        for h in range(STEPS):
            waits[1].append(copy(halos_in[2 * h].at[0], raw.at[-1 - h - low, 1 - odd]))
            waits[1].append(copy(halos_in[2 * h + 1].at[0], raw.at[-1 - h - low, odd]))
    if not stage.first:
        for level in range(1, STEPS + 1):
            waits[level + 1].append(
                copy(carries_in[level - 1], filtered[level].at[pl.ds(0, 2 * sides)])
            )
    for q in range(stage.sensor_high - 1, stage.sensor_low - 1, -1):
        for s in range(2):
            if q < 0:
                side = 1 - odd if s == 0 else odd
                source, target = sensor_halo_in[s].at[-1 - q], sensor.at[q - stage.sensor_low, side]
            else:
                source, target = sensor_in.at[0, planes - 1 - q if s else q], sensor.at[q - stage.sensor_low, s]
            waits[2].append(copy(source, target))
    out_low, out_high = stage.todo[STEPS + 1]
    for q in range(out_low, out_high):
        for s in range(2):
            plane = planes - 1 - q if s else q
            waits[STEPS + 1].append(copy(own_in.at[0, :, plane], own.at[q - out_low, s]))

    blank = jnp.zeros((PAD, LANES), jnp.float32)
    for level in range(1, STEPS + 1):
        skip = 0 if stage.first else 2 * sides
        ref = filtered[level]

        def clear(i, ref=ref):
            for b in range(blocks):
                ref[i, b, 0:PAD] = blank
                ref[i, b, PAD + nth : 2 * PAD + nth] = blank

        pl.loop(skip, ref.shape[0])(clear)

    lane = lax.broadcasted_iota(jnp.int32, (ROWS, LANES), 1)
    at_start = lane == 0
    at_end = lane == LANES - 1
    weight = [[coupling[g, f] for f in range(fields)] for g in range(fields)]

    def put(value, place, row, b):
        at = (pl.ds(pl.multiple_of(row, ROWS), ROWS), slice(b * LANES, (b + 1) * LANES))
        high = value.astype(jnp.bfloat16)
        highs[place][at] = high
        lows[place][at] = (value - high.astype(jnp.float32)).astype(jnp.bfloat16)

    def split_raw(q, place, t):
        slot = q - stage.todo[1][0]
        for s in range(2):
            for f in range(fields):
                for b in range(blocks):
                    value = raw[slot, s, f, pl.ds(t, ROWS), b * LANES : (b + 1) * LANES]
                    put(value, place, (s * fields + f) * nth + t, b)

    def advance(level, q, place, t):
        ref = filtered[level - 1]
        slot = q - stage.base[level - 1]
        row = pl.multiple_of(PAD + t, PAD)
        for s in range(2):
            here = slot * sides + s * fields
            before = here - sides
            after = here + sides if q < stage.half - 1 else slot * sides + (1 - s) * fields
            for b in range(blocks):
                middles, laps = [], []
                for f in range(fields):
                    middle = ref[here + f, b, pl.ds(row, ROWS)]
                    lower = ref[here + f, b - 1, pl.ds(row, ROWS)] if b else 0.0
                    upper = ref[here + f, b + 1, pl.ds(row, ROWS)] if b + 1 < blocks else 0.0
                    left = pltpu.roll(jnp.where(at_end, lower, middle), 1, 1)
                    right = pltpu.roll(jnp.where(at_start, upper, middle), LANES - 1, 1)
                    axial = ref[before + f, b, pl.ds(row, ROWS)] + ref[after + f, b, pl.ds(row, ROWS)]
                    around = ref[here + f, b, pl.ds(PAD + t - 1, ROWS)] + ref[here + f, b, pl.ds(PAD + t + 1, ROWS)]
                    middles.append(middle)
                    laps.append((axial + around) + (left + right) - 6.0 * middle)
                sens = sensor[q - stage.sensor_low, s, pl.ds(t, ROWS), b * LANES : (b + 1) * LANES]
                for f in range(fields):
                    mixed = weight[0][f] * laps[0]
                    for g in range(1, fields):
                        mixed = mixed + weight[g][f] * laps[g]
                    value = middles[f] + sens * mixed
                    if level == STEPS + 1:
                        at = (q - out_low, s, f, pl.ds(t, ROWS), slice(b * LANES, (b + 1) * LANES))
                        own[at] = value - own[at]
                    else:
                        put(value, place, (s * fields + f) * nth + t, b)

    parts = nth // ROWS
    width = weights.shape[-1]

    def project(level, q, place, j):
        ref = filtered[level]
        slot = q - stage.base[level]
        high = highs[place][...]
        left = jnp.concatenate([high, lows[place][...], high], axis=1)
        result = jnp.dot(left, weights[j], preferred_element_type=jnp.float32)
        for i in range(sides):
            for b in range(width // LANES):
                ref[slot * sides + i, j * (width // LANES) + b, PAD : PAD + nth] = result[
                    i * nth : (i + 1) * nth, b * LANES : (b + 1) * LANES
                ]

    def together(task, held):
        def part(j):
            if held is not None:
                project(*held, j)
            if task is not None:
                level, q, place = task
                t = pl.multiple_of(j * ROWS, ROWS)
                if level == 1:
                    split_raw(q, place, t)
                else:
                    advance(level, q, place, t)

        pl.loop(0, parts)(part)

    finish = []

    def carry_out(level):
        if not stage.last:
            ref = filtered[level]
            finish.append(
                copy(ref.at[pl.ds(ref.shape[0] - 2 * sides, 2 * sides)], carries_out[level - 1])
            )

    held = None
    for level in range(1, STEPS + 2):
        for made in waits[level]:
            made.wait()
        for q in range(*stage.todo[level]):
            if held is not None and held[0] == level - 1 and held[1] <= q + 1:
                together(None, held)
                held = None
            place = 0 if held is None else 1 - held[2]
            together((level, q, place), held)
            held = (level, q, place) if level <= STEPS else None
            if level == STEPS + 1:
                for s in range(2):
                    plane = planes - 1 - q if s else q
                    finish.append(copy(own.at[q - out_low, s], out.at[0, :, plane]))
    for level in range(1, STEPS + 1):
        carry_out(level)
    for made in finish:
        made.wait()


def pack(operands, moves, shapes):
    anywhere = pl.BlockSpec(memory_space=pl.ANY)
    plan = [(o, source, len(operands) + result, target) for o, source, result, target in moves]
    return pl.pallas_call(
        functools.partial(pack_kernel, plan),
        out_shape=[jax.ShapeDtypeStruct(shape, jnp.float32) for shape in shapes],
        in_specs=[anywhere] * len(operands),
        out_specs=[anywhere] * len(shapes),
        scratch_shapes=[pltpu.SemaphoreType.DMA((len(plan),))],
        cost_estimate=pl.CostEstimate(
            flops=0, bytes_accessed=8 * sum(math.prod(shape) for shape in shapes), transcendentals=0
        ),
        compiler_params=pltpu.CompilerParams(vmem_limit_bytes=VMEM_MOST),
        name="pack",
    )(*operands)


def run_stage(stage, groups, coupling, odd, weights, own, sensor, chunks, halos, sensor_halos, carries, out):
    fields, planes, nth, nr = own.shape[1:]
    sides = 2 * fields
    blocks = nr // LANES
    held = nth + 2 * PAD
    anywhere = pl.BlockSpec(memory_space=pl.ANY)
    operands = [coupling, odd, weights, own, sensor, *chunks]
    if stage.first:
        operands += [*halos, *sensor_halos]
    else:
        operands += [*carries, out]
    in_specs = [pl.BlockSpec(memory_space=pltpu.SMEM)] * 2 + [anywhere] * (len(operands) - 2)
    out_shape = [jax.ShapeDtypeStruct(own.shape, jnp.float32)]
    if not stage.last:
        out_shape += [jax.ShapeDtypeStruct((2 * sides, blocks, held, LANES), jnp.float32)] * STEPS
    low, high = stage.todo[1]
    outs = stage.todo[STEPS + 1][1] - stage.todo[STEPS + 1][0]
    depths = stage.sensor_high - stage.sensor_low
    copies = 1 + len(chunks) + 2 * STEPS + 2 + STEPS * 2 + 2 * depths + 4 * outs
    scratch = [
        pltpu.VMEM(weights.shape, jnp.bfloat16),
        pltpu.VMEM((outs, 2, fields, nth, nr), jnp.float32),
        pltpu.VMEM((depths, 2, nth, nr), jnp.float32),
        pltpu.VMEM((high - low, 2, fields, nth, nr), jnp.float32),
        *[
            pltpu.VMEM((stage.slots[level] * sides, blocks, held, LANES), jnp.float32)
            for level in range(1, STEPS + 1)
        ],
        *[pltpu.VMEM((sides * nth, nr), jnp.bfloat16)] * 4,
        pltpu.SemaphoreType.DMA((copies,)),
    ]
    limit = VMEM_SPARE + sum(math.prod(s.shape) * s.dtype.itemsize for s in scratch[:-1])
    return pl.pallas_call(
        functools.partial(stage_kernel, stage, fields, planes, groups),
        out_shape=out_shape,
        in_specs=in_specs,
        out_specs=[anywhere] * len(out_shape),
        scratch_shapes=scratch,
        input_output_aliases={} if stage.first else {len(operands) - 1: 0},
        cost_estimate=pl.CostEstimate(flops=0, bytes_accessed=0, transcendentals=0),
        compiler_params=pltpu.CompilerParams(vmem_limit_bytes=limit),
        name=f"stage_{'first' if stage.first else 'last' if stage.last else 'middle'}",
    )(*operands)


def shards(adjoint_in, sensor, filter_matrix, coupling):
    fields, planes, nth, nr = adjoint_in.shape[1:]
    half = planes // 2
    segs = lax.axis_size("seg")
    slabs = lax.axis_size("gx")
    back = [((i + 1) % segs, i) for i in range(segs)]

    groups = []
    for count in GROUPS:
        if sum(groups) + count < half:
            groups.append(count)
    groups.append(half - sum(groups))

    starts = [sum(groups[:i]) for i in range(len(groups))]
    shapes = [(count, 2, fields, nth, nr) for count in groups]
    moves = []
    for i, (start, count) in enumerate(zip(starts, groups)):
        moves.append([])
        for k in range(count):
            for s, plane in enumerate((start + k, planes - 1 - start - k)):
                moves[i].append((0, (0, slice(None), plane), i, (k, s)))
    (first_chunk,) = pack([adjoint_in], moves[0], shapes[:1])
    edge = STEPS - 1
    sensor_moves = [
        (1, (0, plane), len(groups), (k, s))
        for k in range(edge)
        for s, plane in enumerate((k, planes - 1 - k))
    ]
    *rest, sensor_edges = pack(
        [adjoint_in, sensor, first_chunk],
        [(o, a, r - 1, t) for o, a, r, t in sum(moves[1:], []) + sensor_moves],
        shapes[1:] + [(edge, 2, nth, nr)],
    )
    odd = lax.rem(lax.axis_index("gx"), 2)

    def swapped(edges):
        result = []
        for parity in range(2):
            pairs = [(i, i + 1) for i in range(parity, slabs - 1, 2)]
            side = 1 - odd if parity == 0 else odd
            mine = lax.dynamic_index_in_dim(edges, side, 1, keepdims=False)
            result.append(lax.ppermute(mine, "gx", pairs + [(j, i) for i, j in pairs]))
        return result

    high = lax.reduce_precision(filter_matrix, 8, 7)
    low = filter_matrix - high
    weights = jnp.concatenate([high, high, low], axis=0).astype(jnp.bfloat16)
    parts = nth // ROWS
    weights = weights.reshape(STEPS * nr, parts, nr // parts).transpose(1, 0, 2)

    chunks, exchanged = [], []
    for i, packed in enumerate([first_chunk, *rest]):
        if i > 1:
            tied = (packed, weights, chunks[i - 2], *exchanged[i - 2])
            packed, weights, chunks[i - 2], *exchanged[i - 2] = lax.optimization_barrier(tied)
        chunks.append(lax.ppermute(packed, "seg", back))
        if i == 0:
            exchanged.append(swapped(sensor_edges))
        elif i <= STEPS:
            exchanged.append(swapped(chunks[i - 1][:1]))
    sensor_halos, *halos = exchanged
    halos = sum(halos, [])

    odd = odd.astype(jnp.int32)[None]

    cuts = [0, len(groups) - 2, len(groups) - 1, len(groups)]
    carries, out = None, None
    depth = 0
    for low_cut, high_cut in zip(cuts[:-1], cuts[1:]):
        mine = groups[low_cut:high_cut]
        stage = Stage(depth if low_cut else -STEPS, depth + sum(mine), half)
        depth += sum(mine)
        out, *carries = run_stage(
            stage, mine, coupling, odd, weights, adjoint_in, sensor,
            chunks[low_cut:high_cut], halos, sensor_halos, carries, out,
        )
    return out


def solution(mesh):
    in_specs = (P("seg", None, "gx", None, None), P("seg", "gx", None, None), P(), P())
    out_specs = P("seg", None, "gx", None, None)
    return jax.shard_map(shards, mesh=mesh, in_specs=in_specs, out_specs=out_specs, check_vma=False)
```

```python
import functools
import math

import jax
import jax.numpy as jnp
from jax import lax
from jax.experimental import pallas as pl
from jax.experimental.pallas import tpu as pltpu
from jax.sharding import PartitionSpec as P

STEPS = 3
LANES = 128
PAD = 8
ROWS = 16
GROUPS = (1, 1, 1, 1, 1, 1, 1)
TOGETHER = 2
VMEM_SPARE = 6 * 1024 * 1024
VMEM_MOST = 60 * 1024 * 1024


class Stage:
    def __init__(self, start, stop, half):
        self.half = half
        self.first, self.last = start == -STEPS, stop == half
        self.todo = {}
        for level in range(1, STEPS + 2):
            lag = level - 1
            low = start + lag if self.first else start - lag
            self.todo[level] = (low, stop if self.last else stop - lag)
        self.taken, self.given, self.kept = [], [], []
        for level in range(1, STEPS + 1):
            low, high = self.todo[level]
            if not self.first:
                self.taken += [(level, low - 2), (level, low - 1)]
            handed = high if self.last else high - 2
            self.kept += [(level, q) for q in range(low, min(handed, high))]
            self.given += [(level, q) for q in range(max(handed, low), high)]


def pack_first_kernel(planes, source, result, sems):
    made = []
    for s, plane in enumerate((0, planes - 1)):
        made.append(pltpu.make_async_copy(source.at[0, :, plane], result.at[0, s], sems.at[s]))
        made[-1].start()
    for one in made:
        one.wait()


def pack_rest_kernel(planes, groups, source, sensor, first, *results):
    del first
    depth = groups[0]
    for result, count in zip(results, groups[1:]):
        for k in range(count):
            for s, plane in enumerate((depth + k, planes - 1 - depth - k)):

                def field(f, result=result, k=k, s=s, plane=plane):
                    result[k, s, f] = source[0, f, plane]

                pl.loop(0, source.shape[1])(field)
        depth += count
    for k in range(STEPS - 1):
        for s, plane in enumerate((k, planes - 1 - k)):
            results[-1][k, s] = sensor[0, plane]


def stage_kernel(stage, fields, planes, groups, *refs):
    refs = list(refs)

    def take(count):
        got = refs[:count]
        del refs[:count]
        return got

    (coupling, odd_ref, weights, own, sensor) = take(5)
    chunks = take(len(groups))
    halos = take(2 * STEPS) if stage.first else []
    sensor_halos = take(2) if stage.first else []
    filtered = dict(zip(stage.taken, take(len(stage.taken))))
    if not stage.first:
        take(1)
    (out,) = take(1)
    fresh = dict(zip(stage.given, take(len(stage.given))))
    (result,) = take(1)
    fresh.update(zip(stage.kept, take(len(stage.kept))))
    filtered.update(fresh)
    highs = take(2)
    lows = take(2)
    (sems,) = take(1)

    sides = 2 * fields
    nth, nr = own.shape[-2:]
    blocks = nr // LANES
    stride = nth + PAD
    odd = odd_ref[0]

    blank = jnp.zeros((PAD, LANES), jnp.float32)
    for ref in fresh.values():

        def clear(i, ref=ref):
            for b in range(blocks):
                ref[b, pl.ds(pl.multiple_of(i * stride, PAD), PAD)] = blank

        pl.loop(0, sides + 1)(clear)

    lane = lax.broadcasted_iota(jnp.int32, (ROWS, LANES), 1)
    at_start = lane == 0
    at_end = lane == LANES - 1
    weight = [[coupling[g, f] for f in range(fields)] for g in range(fields)]

    def columns(b):
        return slice(b * LANES, (b + 1) * LANES)

    def put(value, place, row, b):
        at = (pl.ds(pl.multiple_of(row, ROWS), ROWS), columns(b))
        high = value.astype(jnp.bfloat16)
        highs[place][at] = high
        lows[place][at] = (value - high.astype(jnp.float32)).astype(jnp.bfloat16)

    def split_raw(q, place, t):
        for s in range(2):
            if q < 0:
                source = halos[2 * (-1 - q) + s].at[0]
                side = 1 - odd if s == 0 else odd
            else:
                chunk, k = starts[q]
                source, side = chunks[chunk].at[k, s], s
            for f in range(fields):
                for b in range(blocks):
                    put(source[f, pl.ds(t, ROWS), columns(b)], place, (side * fields + f) * nth + t, b)

    def sensor_at(q, s, t, b):
        if q >= 0:
            return sensor[0, planes - 1 - q if s else q, pl.ds(t, ROWS), columns(b)]
        pair = [ref[-1 - q, pl.ds(t, ROWS), columns(b)] for ref in sensor_halos]
        return jnp.where(odd == s, pair[1], pair[0])

    def advance(level, q, place, t):
        here = filtered[level - 1, q]
        before = filtered[level - 1, q - 1]
        inner = q < stage.half - 1
        after = filtered[level - 1, q + 1] if inner else here
        for s in range(2):
            rows = [(s * fields + f) * stride + PAD + t for f in range(fields)]
            beyond = rows if inner else [((1 - s) * fields + f) * stride + PAD + t for f in range(fields)]
            aligned = [pl.ds(pl.multiple_of(row, PAD), ROWS) for row in rows]
            beyond = [pl.ds(pl.multiple_of(row, PAD), ROWS) for row in beyond]
            middles = [[here[b, aligned[f]] for b in range(blocks)] for f in range(fields)]
            for b in range(blocks):
                laps = []
                for f in range(fields):
                    middle = middles[f][b]
                    lower = middles[f][b - 1] if b else 0.0
                    upper = middles[f][b + 1] if b + 1 < blocks else 0.0
                    left = pltpu.roll(jnp.where(at_end, lower, middle), 1, 1)
                    right = pltpu.roll(jnp.where(at_start, upper, middle), LANES - 1, 1)
                    axial = before[b, aligned[f]] + after[b, beyond[f]]
                    around = here[b, pl.ds(rows[f] - 1, ROWS)] + here[b, pl.ds(rows[f] + 1, ROWS)]
                    laps.append((axial + around) + (left + right) - 6.0 * middle)
                sens = sensor_at(q, s, t, b)
                for f in range(fields):
                    mixed = weight[0][f] * laps[0]
                    for g in range(1, fields):
                        mixed = mixed + weight[g][f] * laps[g]
                    value = middles[f][b] + sens * mixed
                    if level == STEPS + 1:
                        plane = planes - 1 - q if s else q
                        at = (pl.ds(t, ROWS), columns(b))
                        result[(q - out_low, s, f, *at)] = value - own[(0, f, plane, *at)]
                    else:
                        put(value, place, (s * fields + f) * nth + t, b)

    starts = {}
    depth = max(stage.todo[1][0], 0)
    for i, count in enumerate(groups):
        for k in range(count):
            starts[depth] = (i, k)
            depth += 1
    out_low = stage.todo[STEPS + 1][0]
    parts = nth // ROWS
    width = weights.shape[-1]

    def project(level, q, place, j):
        ref = filtered[level, q]
        high = highs[place][...]
        left = jnp.concatenate([high, lows[place][...], high], axis=1)
        product = jnp.dot(left, weights[j], preferred_element_type=jnp.float32)
        for i in range(sides):
            for b in range(width // LANES):
                ref[j * (width // LANES) + b, i * stride + PAD : (i + 1) * stride] = product[
                    i * nth : (i + 1) * nth, columns(b)
                ]

    def together(task, held):
        def part(j):
            if held is not None:
                project(*held, j)
            if task is not None:
                level, q, place = task
                t = pl.multiple_of(j * ROWS, ROWS)
                if level == 1:
                    split_raw(q, place, t)
                else:
                    advance(level, q, place, t)

        pl.loop(0, parts)(part)

    held = None
    sent = []
    for level in range(1, STEPS + 2):
        for q in range(*stage.todo[level]):
            if held is not None and held[0] == level - 1 and held[1] <= q + 1:
                together(None, held)
                held = None
            place = 0 if held is None else 1 - held[2]
            together((level, q, place), held)
            held = (level, q, place) if level <= STEPS else None
            if level == STEPS + 1:
                for s in range(2):
                    plane = planes - 1 - q if s else q
                    sent.append(
                        pltpu.make_async_copy(result.at[q - out_low, s], out.at[0, :, plane], sems.at[len(sent)])
                    )
                    sent[-1].start()
    if held is not None:
        together(None, held)
    for made in sent:
        made.wait()


ANYWHERE = pl.BlockSpec(memory_space=pl.ANY)
CLOSE = pl.BlockSpec(memory_space=pltpu.VMEM)
SCALARS = pl.BlockSpec(memory_space=pltpu.SMEM)


def size(*arrays):
    return sum(math.prod(array.shape) * array.dtype.itemsize for array in arrays)


def pack_first(adjoint_in):
    fields, planes, nth, nr = adjoint_in.shape[1:]
    return pl.pallas_call(
        functools.partial(pack_first_kernel, planes),
        out_shape=jax.ShapeDtypeStruct((1, 2, fields, nth, nr), jnp.float32),
        in_specs=[ANYWHERE],
        out_specs=CLOSE,
        scratch_shapes=[pltpu.SemaphoreType.DMA((2,))],
        compiler_params=pltpu.CompilerParams(vmem_limit_bytes=VMEM_MOST),
        name="pack_first",
    )(adjoint_in)


def pack_rest(adjoint_in, sensor, first, groups):
    fields, planes, nth, nr = adjoint_in.shape[1:]
    shapes = [(count, 2, fields, nth, nr) for count in groups[1:]] + [(STEPS - 1, 2, nth, nr)]
    out_shape = [jax.ShapeDtypeStruct(shape, jnp.float32) for shape in shapes]
    return pl.pallas_call(
        functools.partial(pack_rest_kernel, planes, groups),
        out_shape=out_shape,
        in_specs=[CLOSE, CLOSE, ANYWHERE],
        out_specs=[CLOSE] * len(shapes),
        cost_estimate=pl.CostEstimate(flops=0, bytes_accessed=2 * size(*out_shape), transcendentals=0),
        compiler_params=pltpu.CompilerParams(
            vmem_limit_bytes=VMEM_SPARE + size(adjoint_in, sensor, *out_shape)
        ),
        name="pack_rest",
    )(adjoint_in, sensor, first)


def run_stage(stage, groups, coupling, odd, weights, own, sensor, chunks, halos, sensor_halos, carried, out):
    fields, planes, nth, nr = own.shape[1:]
    sides = 2 * fields
    slot = (nr // LANES, sides * (nth + PAD) + PAD, LANES)
    close = [weights, own, sensor, *chunks]
    if stage.first:
        close += [*halos, *sensor_halos]
    close += [carried[key] for key in stage.taken]
    operands = [coupling, odd, *close] + ([] if stage.first else [out])
    in_specs = [SCALARS] * 2 + [CLOSE] * len(close) + ([] if stage.first else [ANYWHERE])
    given = [jax.ShapeDtypeStruct(slot, jnp.float32)] * len(stage.given)
    low, high = stage.todo[STEPS + 1]
    scratch = [
        pltpu.VMEM((high - low, 2, fields, nth, nr), jnp.float32),
        *[pltpu.VMEM(slot, jnp.float32)] * len(stage.kept),
        *[pltpu.VMEM((sides * nth, nr), jnp.bfloat16)] * 4,
    ]
    limit = VMEM_SPARE + size(*scratch, *close, *given)
    out, *fresh = pl.pallas_call(
        functools.partial(stage_kernel, stage, fields, planes, groups),
        out_shape=[jax.ShapeDtypeStruct(own.shape, jnp.float32), *given],
        in_specs=in_specs,
        out_specs=[ANYWHERE] + [CLOSE] * len(given),
        scratch_shapes=scratch + [pltpu.SemaphoreType.DMA((2 * max(high - low, 1),))],
        input_output_aliases={} if stage.first else {len(operands) - 1: 0},
        cost_estimate=pl.CostEstimate(
            flops=0, bytes_accessed=size(*close, *given) if stage.first else 0, transcendentals=0
        ),
        compiler_params=pltpu.CompilerParams(vmem_limit_bytes=limit),
        name=f"stage_{'first' if stage.first else 'last' if stage.last else 'middle'}",
    )(*operands)
    return out, dict(zip(stage.given, fresh))


def shards(adjoint_in, sensor, filter_matrix, coupling):
    fields, planes, nth, nr = adjoint_in.shape[1:]
    half = planes // 2
    segs = lax.axis_size("seg")
    slabs = lax.axis_size("gx")
    back = [((i + 1) % segs, i) for i in range(segs)]

    groups = []
    for count in GROUPS:
        if sum(groups) + count < half:
            groups.append(count)
    groups.append(half - sum(groups))

    first_chunk = pack_first(adjoint_in)
    *rest, sensor_edges = pack_rest(adjoint_in, sensor, first_chunk, groups)

    odd = lax.rem(lax.axis_index("gx"), 2)

    def swapped(edges):
        result = []
        for parity in range(2):
            pairs = [(i, i + 1) for i in range(parity, slabs - 1, 2)]
            side = 1 - odd if parity == 0 else odd
            mine = lax.dynamic_index_in_dim(edges, side, 1, keepdims=False)
            result.append(lax.ppermute(mine, "gx", pairs + [(j, i) for i, j in pairs]))
        return result

    high = lax.reduce_precision(filter_matrix, 8, 7)
    low = filter_matrix - high
    parts = nth // ROWS
    weights = [
        jnp.concatenate([high[:, at], high[:, at], low[:, at]], axis=0)
        for at in (slice(j * (nr // parts), (j + 1) * (nr // parts)) for j in range(parts))
    ]
    weights = jnp.stack(weights).astype(jnp.bfloat16)
    scalar = odd.astype(jnp.int32)[None]

    stages = [(0, STEPS)]
    while stages[-1][1] < len(groups):
        low_cut = stages[-1][1]
        stages.append((low_cut, max(min(low_cut + TOGETHER, len(groups) - 1), low_cut + 1)))
    cuts = [sum(groups[:i]) for i in range(len(groups) + 1)]
    carried, out = {}, None
    halos, sensor_halos = [], []

    def run(number):
        nonlocal out
        low_cut, high_cut = stages[number]
        mine = groups[low_cut:high_cut]
        stage = Stage(cuts[low_cut] if number else -STEPS, cuts[high_cut], half)
        out, fresh = run_stage(
            stage, mine, coupling, scalar, weights, adjoint_in, sensor,
            chunks[low_cut:high_cut], halos, sensor_halos, carried, out,
        )
        carried.update(fresh)

    chunks, exchanged = [], []
    ran = 0

    def unpack():
        nonlocal sensor_halos, halos
        sensor_halos, *halos = exchanged
        halos = sum(halos, [])

    for i, packed in enumerate([first_chunk, *rest]):
        if i >= STEPS + 3 and stages[ran][1] < i:
            if ran == 0:
                unpack()
            run(ran)
            ran += 1
            key = max(carried)
            packed, carried[key] = lax.optimization_barrier((packed, carried[key]))
        elif i > 1:
            ends = exchanged[i - 2] if i - 2 < len(exchanged) else []
            packed, weights, chunks[i - 2], *ends = lax.optimization_barrier((packed, weights, chunks[i - 2], *ends))
            if ends:
                exchanged[i - 2] = ends
        chunks.append(lax.ppermute(packed, "seg", back))
        if i == 0:
            exchanged.append(swapped(sensor_edges))
        elif i <= STEPS:
            exchanged.append(swapped(chunks[i - 1][:1]))
    for number in range(ran, len(stages)):
        if number == 0:
            unpack()
        run(number)
    return out


def solution(mesh):
    in_specs = (P("seg", None, "gx", None, None), P("seg", "gx", None, None), P(), P())
    out_specs = P("seg", None, "gx", None, None)
    return jax.shard_map(shards, mesh=mesh, in_specs=in_specs, out_specs=out_specs, check_vma=False)
```

```python
import functools
import math

import jax
import jax.numpy as jnp
from jax import lax
from jax.experimental import pallas as pl
from jax.experimental.pallas import tpu as pltpu
from jax.sharding import PartitionSpec as P

STEPS = 3
LANES = 128
PAD = 8
ROWS = 16
GROUPS = (1, 1, 1, 1, 1, 1, 1)
TOGETHER = 2
VMEM_SPARE = 6 * 1024 * 1024
VMEM_MOST = 60 * 1024 * 1024


class Stage:
    def __init__(self, start, stop, half):
        self.half = half
        self.first, self.last = start == -STEPS, stop == half
        self.todo = {}
        for level in range(1, STEPS + 2):
            lag = level - 1
            low = start + lag if self.first else start - lag
            self.todo[level] = (low, stop if self.last else stop - lag)
        self.taken, self.given, self.kept = [], [], []
        for level in range(1, STEPS + 1):
            low, high = self.todo[level]
            if not self.first:
                self.taken += [(level, low - 2), (level, low - 1)]
            handed = high if self.last else high - 2
            self.kept += [(level, q) for q in range(low, min(handed, high))]
            self.given += [(level, q) for q in range(max(handed, low), high)]


def pack_first_kernel(planes, source, result, sems):
    made = []
    for s, plane in enumerate((0, planes - 1)):
        made.append(pltpu.make_async_copy(source.at[0, :, plane], result.at[0, s], sems.at[s]))
        made[-1].start()
    for one in made:
        one.wait()


def pack_rest_kernel(planes, groups, source, sensor, first, *refs):
    del first
    *results, held, edges, sems = refs
    plan = []
    depth = groups[0]
    for result, count in zip(results, groups[1:]):
        for k in range(count):
            place = held.at[depth - groups[0] + k]
            plan.append(
                ([(source.at[0, :, depth + k], place.at[0]), (source.at[0, :, planes - 1 - depth - k], place.at[1])],
                 place, result.at[k])
            )
        depth += count
    ends = [
        (sensor.at[0, plane], edges.at[k, s])
        for k in range(STEPS - 1)
        for s, plane in enumerate((k, planes - 1 - k))
    ]
    plan.append((ends, edges, results[-1]))
    count = 0

    def start(source, target):
        nonlocal count
        made = pltpu.make_async_copy(source, target, sems.at[count])
        count += 1
        made.start()
        return made

    inward = [[start(*pair) for pair in pairs] for pairs, _, _ in plan]
    outward = []
    for made, (_, place, result) in zip(inward, plan):
        for one in made:
            one.wait()
        outward.append(start(place, result))
    for one in outward:
        one.wait()


def stage_kernel(stage, fields, planes, groups, *refs):
    refs = list(refs)

    def take(count):
        got = refs[:count]
        del refs[:count]
        return got

    (coupling, odd_ref, weights, own, sensor) = take(5)
    chunks = take(len(groups))
    halos = take(2 * STEPS) if stage.first else []
    filtered = dict(zip(stage.taken, take(len(stage.taken))))
    if not stage.first:
        take(1)
    (out,) = take(1)
    fresh = dict(zip(stage.given, take(len(stage.given))))
    (result,) = take(1)
    fresh.update(zip(stage.kept, take(len(stage.kept))))
    filtered.update(fresh)
    highs = take(2)
    lows = take(2)
    (sems,) = take(1)

    sides = 2 * fields
    nth, nr = own.shape[-2:]
    blocks = nr // LANES
    stride = nth + PAD
    odd, base = odd_ref[0], odd_ref[1]

    blank = jnp.zeros((PAD, LANES), jnp.float32)
    for ref in fresh.values():

        def clear(i, ref=ref):
            for b in range(blocks):
                ref[b, pl.ds(pl.multiple_of(i * stride, PAD), PAD)] = blank

        pl.loop(0, sides + 1)(clear)

    lane = lax.broadcasted_iota(jnp.int32, (ROWS, LANES), 1)
    at_start = lane == 0
    at_end = lane == LANES - 1
    weight = [[coupling[g, f] for f in range(fields)] for g in range(fields)]

    def columns(b):
        return slice(b * LANES, (b + 1) * LANES)

    def put(value, place, row, b):
        at = (pl.ds(pl.multiple_of(row, ROWS), ROWS), columns(b))
        high = value.astype(jnp.bfloat16)
        highs[place][at] = high
        lows[place][at] = (value - high.astype(jnp.float32)).astype(jnp.bfloat16)

    def split_raw(q, place, t):
        for s in range(2):
            if q < 0:
                source = halos[2 * (-1 - q) + s]
                side = 1 - odd if s == 0 else odd
            else:
                chunk, k = starts[q]
                source, side = chunks[chunk].at[k, s], s
            for f in range(fields):
                for b in range(blocks):
                    put(source[f, pl.ds(t, ROWS), columns(b)], place, (side * fields + f) * nth + t, b)

    def sensor_at(q, s, t, b):
        if q >= 0:
            return sensor[0, planes - 1 - q if s else q, pl.ds(t, ROWS), columns(b)]
        pair = [ref[fields, pl.ds(t, ROWS), columns(b)] for ref in halos[2 * (-1 - q) : 2 * (-q)]]
        return jnp.where(odd == s, pair[1], pair[0])

    def advance(level, q, place, t):
        here = filtered[level - 1, q]
        before = filtered[level - 1, q - 1]
        inner = q < stage.half - 1
        after = filtered[level - 1, q + 1] if inner else here
        for s in range(2):
            rows = [(s * fields + f) * stride + PAD + t for f in range(fields)]
            beyond = rows if inner else [((1 - s) * fields + f) * stride + PAD + t for f in range(fields)]
            aligned = [pl.ds(pl.multiple_of(row, PAD), ROWS) for row in rows]
            beyond = [pl.ds(pl.multiple_of(row, PAD), ROWS) for row in beyond]
            middles = [[here[b, aligned[f]] for b in range(blocks)] for f in range(fields)]
            for b in range(blocks):
                laps = []
                for f in range(fields):
                    middle = middles[f][b]
                    lower = middles[f][b - 1] if b else 0.0
                    upper = middles[f][b + 1] if b + 1 < blocks else 0.0
                    left = pltpu.roll(jnp.where(at_end, lower, middle), 1, 1)
                    right = pltpu.roll(jnp.where(at_start, upper, middle), LANES - 1, 1)
                    axial = before[b, aligned[f]] + after[b, beyond[f]]
                    around = here[b, pl.ds(base + (rows[f] - 1), ROWS)] + here[b, pl.ds(base + (rows[f] + 1), ROWS)]
                    laps.append((axial + around) + (left + right) - 6.0 * middle)
                sens = sensor_at(q, s, t, b)
                for f in range(fields):
                    mixed = weight[0][f] * laps[0]
                    for g in range(1, fields):
                        mixed = mixed + weight[g][f] * laps[g]
                    value = middles[f][b] + sens * mixed
                    if level == STEPS + 1:
                        plane = planes - 1 - q if s else q
                        at = (pl.ds(t, ROWS), columns(b))
                        result[(q - out_low, s, f, *at)] = value - own[(0, f, plane, *at)]
                    else:
                        put(value, place, (s * fields + f) * nth + t, b)

    starts = {}
    depth = max(stage.todo[1][0], 0)
    for i, count in enumerate(groups):
        for k in range(count):
            starts[depth] = (i, k)
            depth += 1
    out_low = stage.todo[STEPS + 1][0]

    def project(level, q, place):
        ref = filtered[level, q]
        high = highs[place][...]
        left = jnp.concatenate([high, lows[place][...], high], axis=1)
        product = jnp.dot(left, weights[...], preferred_element_type=jnp.float32)
        for i in range(sides):
            for b in range(blocks):
                ref[b, i * stride + PAD : (i + 1) * stride] = product[i * nth : (i + 1) * nth, columns(b)]

    def together(task, held):
        if held is not None:
            project(*held)
        if task is not None:
            level, q, place = task
            for t in range(0, nth, ROWS):
                if level == 1:
                    split_raw(q, place, t)
                else:
                    advance(level, q, place, t)

    held = None
    sent = []
    for level in range(1, STEPS + 2):
        for q in range(*stage.todo[level]):
            if held is not None and held[0] == level - 1 and held[1] <= q + 1:
                together(None, held)
                held = None
            place = 0 if held is None else 1 - held[2]
            together((level, q, place), held)
            held = (level, q, place) if level <= STEPS else None
            if level == STEPS + 1:
                for s in range(2):
                    plane = planes - 1 - q if s else q
                    sent.append(
                        pltpu.make_async_copy(result.at[q - out_low, s], out.at[0, :, plane], sems.at[len(sent)])
                    )
                    sent[-1].start()
    if held is not None:
        together(None, held)
    for made in sent:
        made.wait()


ANYWHERE = pl.BlockSpec(memory_space=pl.ANY)
CLOSE = pl.BlockSpec(memory_space=pltpu.VMEM)
SCALARS = pl.BlockSpec(memory_space=pltpu.SMEM)


def size(*arrays):
    return sum(math.prod(array.shape) * array.dtype.itemsize for array in arrays)


def pack_first(adjoint_in):
    fields, planes, nth, nr = adjoint_in.shape[1:]
    return pl.pallas_call(
        functools.partial(pack_first_kernel, planes),
        out_shape=jax.ShapeDtypeStruct((1, 2, fields, nth, nr), jnp.float32),
        in_specs=[ANYWHERE],
        out_specs=CLOSE,
        scratch_shapes=[pltpu.SemaphoreType.DMA((2,))],
        compiler_params=pltpu.CompilerParams(vmem_limit_bytes=VMEM_MOST),
        name="pack_first",
    )(adjoint_in)


def pack_rest(adjoint_in, sensor, first, groups):
    fields, planes, nth, nr = adjoint_in.shape[1:]
    depths = sum(groups[1:])
    edges = (STEPS - 1, 2, nth, nr)
    shapes = [(count, 2, fields, nth, nr) for count in groups[1:]] + [edges]
    out_shape = [jax.ShapeDtypeStruct(shape, jnp.float32) for shape in shapes]
    return pl.pallas_call(
        functools.partial(pack_rest_kernel, planes, groups),
        out_shape=out_shape,
        in_specs=[ANYWHERE] * 3,
        out_specs=[ANYWHERE] * len(shapes),
        scratch_shapes=[
            pltpu.VMEM((depths, 2, fields, nth, nr), jnp.float32),
            pltpu.VMEM(edges, jnp.float32),
            pltpu.SemaphoreType.DMA((3 * depths + 2 * STEPS,)),
        ],
        cost_estimate=pl.CostEstimate(flops=0, bytes_accessed=2 * size(*out_shape), transcendentals=0),
        compiler_params=pltpu.CompilerParams(vmem_limit_bytes=VMEM_MOST),
        name="pack_rest",
    )(adjoint_in, sensor, first)


def run_stage(stage, groups, coupling, odd, weights, own, sensor, chunks, halos, carried, out):
    fields, planes, nth, nr = own.shape[1:]
    sides = 2 * fields
    slot = (nr // LANES, sides * (nth + PAD) + PAD, LANES)
    close = [weights, own, sensor, *chunks]
    if stage.first:
        close += halos
    close += [carried[key] for key in stage.taken]
    operands = [coupling, odd, *close] + ([] if stage.first else [out])
    in_specs = [SCALARS] * 2 + [CLOSE] * len(close) + ([] if stage.first else [ANYWHERE])
    given = [jax.ShapeDtypeStruct(slot, jnp.float32)] * len(stage.given)
    low, high = stage.todo[STEPS + 1]
    scratch = [
        pltpu.VMEM((high - low, 2, fields, nth, nr), jnp.float32),
        *[pltpu.VMEM(slot, jnp.float32)] * len(stage.kept),
        *[pltpu.VMEM((sides * nth, nr), jnp.bfloat16)] * 4,
    ]
    limit = VMEM_SPARE + size(*scratch, *close, *given)
    out, *fresh = pl.pallas_call(
        functools.partial(stage_kernel, stage, fields, planes, groups),
        out_shape=[jax.ShapeDtypeStruct(own.shape, jnp.float32), *given],
        in_specs=in_specs,
        out_specs=[ANYWHERE] + [CLOSE] * len(given),
        scratch_shapes=scratch + [pltpu.SemaphoreType.DMA((2 * max(high - low, 1),))],
        input_output_aliases={} if stage.first else {len(operands) - 1: 0},
        cost_estimate=pl.CostEstimate(
            flops=0, bytes_accessed=size(*close, *given) if stage.first else 0, transcendentals=0
        ),
        compiler_params=pltpu.CompilerParams(vmem_limit_bytes=limit),
        name=f"stage_{'first' if stage.first else 'last' if stage.last else 'middle'}",
    )(*operands)
    return out, dict(zip(stage.given, fresh))


def shards(adjoint_in, sensor, filter_matrix, coupling):
    fields, planes, nth, nr = adjoint_in.shape[1:]
    half = planes // 2
    segs = lax.axis_size("seg")
    slabs = lax.axis_size("gx")
    back = [((i + 1) % segs, i) for i in range(segs)]

    groups = []
    for count in GROUPS:
        if sum(groups) + count < half:
            groups.append(count)
    groups.append(half - sum(groups))

    first_chunk = pack_first(adjoint_in)
    *rest, sensor_edges = pack_rest(adjoint_in, sensor, first_chunk, groups)

    odd = lax.rem(lax.axis_index("gx"), 2)

    def swapped(edges):
        result = []
        for parity in range(2):
            pairs = [(i, i + 1) for i in range(parity, slabs - 1, 2)]
            side = 1 - odd if parity == 0 else odd
            mine = jnp.concatenate([lax.dynamic_index_in_dim(part, side, 0, keepdims=False) for part in edges])
            result.append(lax.ppermute(mine, "gx", pairs + [(j, i) for i, j in pairs]))
        return result

    high = lax.reduce_precision(filter_matrix, 8, 7)
    low = filter_matrix - high
    weights = jnp.concatenate([high, high, low], axis=0).astype(jnp.bfloat16)
    scalar = jnp.stack([odd, 0 * odd]).astype(jnp.int32)

    stages = [(0, STEPS)]
    while stages[-1][1] < len(groups):
        low_cut = stages[-1][1]
        stages.append((low_cut, max(min(low_cut + TOGETHER, len(groups) - 1), low_cut + 1)))
    cuts = [sum(groups[:i]) for i in range(len(groups) + 1)]
    carried, out = {}, None
    halos = []

    def run(number):
        nonlocal out
        low_cut, high_cut = stages[number]
        mine = groups[low_cut:high_cut]
        stage = Stage(cuts[low_cut] if number else -STEPS, cuts[high_cut], half)
        out, fresh = run_stage(
            stage, mine, coupling, scalar, weights, adjoint_in, sensor,
            chunks[low_cut:high_cut], halos, carried, out,
        )
        carried.update(fresh)

    chunks, exchanged = [], []
    ran = 0

    def unpack():
        nonlocal halos
        halos = sum(exchanged, [])

    for i, packed in enumerate([first_chunk, *rest]):
        if i >= STEPS + 3 and stages[ran][1] < i:
            if ran == 0:
                unpack()
            run(ran)
            ran += 1
            key = max(carried)
            packed, carried[key] = lax.optimization_barrier((packed, carried[key]))
        elif i > 1:
            ends = exchanged[i - STEPS] if STEPS <= i < len(exchanged) + STEPS else []
            packed, weights, chunks[i - 2], *ends = lax.optimization_barrier((packed, weights, chunks[i - 2], *ends))
            if ends:
                exchanged[i - STEPS] = ends
        chunks.append(lax.ppermute(packed, "seg", back))
        if 1 <= i <= STEPS:
            edges = [chunks[i - 1][0]] + ([sensor_edges[i - 1][:, None]] if i < STEPS else [])
            exchanged.append(swapped(edges))
    for number in range(ran, len(stages)):
        if number == 0:
            unpack()
        run(number)
    return out


def solution(mesh):
    in_specs = (P("seg", None, "gx", None, None), P("seg", "gx", None, None), P(), P())
    out_specs = P("seg", None, "gx", None, None)
    return jax.shard_map(shards, mesh=mesh, in_specs=in_specs, out_specs=out_specs, check_vma=False)
```

```python
import functools
import math

import jax
import jax.numpy as jnp
from jax import lax
from jax.experimental import pallas as pl
from jax.experimental.pallas import tpu as pltpu
from jax.sharding import PartitionSpec as P

STEPS = 3
LANES = 128
PAD = 8
LATE = 1
ROWS = 16
GROUPS = (1, 1, 1, 1, 1, 1, 1)
TOGETHER = 2
VMEM_SPARE = 6 * 1024 * 1024
VMEM_MOST = 60 * 1024 * 1024


class Stage:
    def __init__(self, start, stop, half):
        self.half = half
        self.first, self.last = start == -STEPS, stop == half
        self.todo = {}
        for level in range(1, STEPS + 2):
            lag = level - 1
            low = start + lag if self.first else start - lag
            self.todo[level] = (low, stop if self.last else stop - lag)
        self.taken, self.given, self.kept = [], [], []
        for level in range(1, STEPS + 1):
            low, high = self.todo[level]
            if not self.first:
                self.taken += [(level, low - 2), (level, low - 1)]
            handed = high if self.last else high - 2
            self.kept += [(level, q) for q in range(low, min(handed, high))]
            self.given += [(level, q) for q in range(max(handed, low), high)]


def pack_first_kernel(planes, source, result, sems):
    made = []
    for s, plane in enumerate((0, planes - 1)):
        made.append(pltpu.make_async_copy(source.at[0, :, plane], result.at[0, s], sems.at[s]))
        made[-1].start()
    for one in made:
        one.wait()


def pack_rest_kernel(planes, groups, source, sensor, first, *refs):
    del first
    *results, held, edges, sems = refs
    plan = []
    depth = groups[0]
    for result, count in zip(results, groups[1:]):
        for k in range(count):
            place = held.at[depth - groups[0] + k]
            plan.append(
                ([(source.at[0, :, depth + k], place.at[0]), (source.at[0, :, planes - 1 - depth - k], place.at[1])],
                 place, result.at[k])
            )
        depth += count
    ends = [
        (sensor.at[0, plane], edges.at[k, s])
        for k in range(STEPS - 1)
        for s, plane in enumerate((k, planes - 1 - k))
    ]
    plan.append((ends, edges, results[-1]))
    count = 0

    def start(source, target):
        nonlocal count
        made = pltpu.make_async_copy(source, target, sems.at[count])
        count += 1
        made.start()
        return made

    inward = [[start(*pair) for pair in pairs] for pairs, _, _ in plan]
    outward = []
    for made, (_, place, result) in zip(inward, plan):
        for one in made:
            one.wait()
        outward.append(start(place, result))
    for one in outward:
        one.wait()


def stage_kernel(stage, fields, planes, groups, *refs):
    refs = list(refs)

    def take(count):
        got = refs[:count]
        del refs[:count]
        return got

    (coupling, odd_ref, weights_in, own, sensor) = take(5)
    chunks = take(len(groups))
    halos = take(2 * STEPS) if stage.first else []
    filtered = dict(zip(stage.taken, take(len(stage.taken))))
    if not stage.first:
        take(1)
    (out,) = take(1)
    fresh = dict(zip(stage.given, take(len(stage.given))))
    (result, weights) = take(2)
    fresh.update(zip(stage.kept, take(len(stage.kept))))
    filtered.update(fresh)
    highs = take(2)
    lows = take(2)
    (sems,) = take(1)

    sides = 2 * fields
    nth, nr = own.shape[-2:]
    blocks = nr // LANES
    stride = nth + PAD
    odd, base = odd_ref[0], odd_ref[1]

    blank = jnp.zeros((PAD, LANES), jnp.float32)
    for ref in fresh.values():

        def clear(i, ref=ref):
            for b in range(blocks):
                ref[b, pl.ds(pl.multiple_of(i * stride, PAD), PAD)] = blank

        pl.loop(0, sides + 1)(clear)

    step = 4 * ROWS

    def fetch(i):
        at = pl.ds(pl.multiple_of(i * step, step), step)
        weights[at] = weights_in[at]

    pl.loop(0, weights.shape[0] // step)(fetch)

    lane = lax.broadcasted_iota(jnp.int32, (ROWS, LANES), 1)
    at_start = lane == 0
    at_end = lane == LANES - 1
    weight = [[coupling[g, f] for f in range(fields)] for g in range(fields)]

    def columns(b):
        return slice(b * LANES, (b + 1) * LANES)

    waiting = []

    def store_late(stores=None):
        if stores is not None:
            waiting.append(stores)
        while len(waiting) > (LATE if stores is not None else 0):
            for store in waiting.pop(0):
                store()

    def put(value, place, row, b):
        at = (pl.ds(pl.multiple_of(row, ROWS), ROWS), columns(b))
        high = value.astype(jnp.bfloat16)
        highs[place][at] = high
        lows[place][at] = (value - high.astype(jnp.float32)).astype(jnp.bfloat16)

    def keep(value, at):
        result[at] = value

    def split_raw(q, place, t):
        for s in range(2):
            if q < 0:
                source = halos[2 * (-1 - q) + s]
                side = 1 - odd if s == 0 else odd
            else:
                chunk, k = starts[q]
                source, side = chunks[chunk].at[k, s], s
            for f in range(fields):
                stores = []
                for b in range(blocks):
                    value = source[f, pl.ds(t, ROWS), columns(b)]
                    stores.append(functools.partial(put, value, place, (side * fields + f) * nth + t, b))
                store_late(stores)

    def sensor_at(q, s, t, b):
        if q >= 0:
            return sensor[0, planes - 1 - q if s else q, pl.ds(t, ROWS), columns(b)]
        pair = [ref[fields, pl.ds(t, ROWS), columns(b)] for ref in halos[2 * (-1 - q) : 2 * (-q)]]
        return jnp.where(odd == s, pair[1], pair[0])

    def advance(level, q, place, t):
        here = filtered[level - 1, q]
        before = filtered[level - 1, q - 1]
        inner = q < stage.half - 1
        after = filtered[level - 1, q + 1] if inner else here
        for s in range(2):
            rows = [(s * fields + f) * stride + PAD + t for f in range(fields)]
            beyond = rows if inner else [((1 - s) * fields + f) * stride + PAD + t for f in range(fields)]
            aligned = [pl.ds(pl.multiple_of(row, PAD), ROWS) for row in rows]
            beyond = [pl.ds(pl.multiple_of(row, PAD), ROWS) for row in beyond]
            middles = [[here[b, aligned[f]] for b in range(blocks)] for f in range(fields)]
            for b in range(blocks):
                laps = []
                for f in range(fields):
                    middle = middles[f][b]
                    lower = middles[f][b - 1] if b else 0.0
                    upper = middles[f][b + 1] if b + 1 < blocks else 0.0
                    left = pltpu.roll(jnp.where(at_end, lower, middle), 1, 1)
                    right = pltpu.roll(jnp.where(at_start, upper, middle), LANES - 1, 1)
                    axial = before[b, aligned[f]] + after[b, beyond[f]]
                    around = here[b, pl.ds(base + (rows[f] - 1), ROWS)] + here[b, pl.ds(base + (rows[f] + 1), ROWS)]
                    laps.append((axial + around) + (left + right) - 6.0 * middle)
                sens = sensor_at(q, s, t, b)
                stores = []
                for f in range(fields):
                    mixed = weight[0][f] * laps[0]
                    for g in range(1, fields):
                        mixed = mixed + weight[g][f] * laps[g]
                    value = middles[f][b] + sens * mixed
                    if level == STEPS + 1:
                        plane = planes - 1 - q if s else q
                        at = (pl.ds(t, ROWS), columns(b))
                        value = value - own[(0, f, plane, *at)]
                        stores.append(functools.partial(keep, value, (q - out_low, s, f, *at)))
                    else:
                        stores.append(functools.partial(put, value, place, (s * fields + f) * nth + t, b))
                store_late(stores)

    starts = {}
    depth = max(stage.todo[1][0], 0)
    for i, count in enumerate(groups):
        for k in range(count):
            starts[depth] = (i, k)
            depth += 1
    out_low = stage.todo[STEPS + 1][0]

    parts = nth // ROWS
    width = nr // parts

    def project(level, q, place, j):
        high = highs[place][...]
        left = jnp.concatenate([high, lows[place][...], high], axis=1)
        return jnp.dot(left, weights[:, j * width : (j + 1) * width], preferred_element_type=jnp.float32)

    def hold(level, q, product, j):
        for i in range(sides):
            for b in range(width // LANES):
                at = (j * (width // LANES) + b, slice(i * stride + PAD, (i + 1) * stride))
                filtered[level, q][at] = product[i * nth : (i + 1) * nth, columns(b)]

    def together(task, held):
        for j in range(parts):
            product = None if held is None else project(*held, j)
            if task is not None:
                level, q, place = task
                if level == 1:
                    split_raw(q, place, j * ROWS)
                else:
                    advance(level, q, place, j * ROWS)
                store_late()
            if held is not None:
                hold(held[0], held[1], product, j)

    held = None
    sent = []
    for level in range(1, STEPS + 2):
        for q in range(*stage.todo[level]):
            if held is not None and held[0] == level - 1 and held[1] <= q + 1:
                together(None, held)
                held = None
            place = 0 if held is None else 1 - held[2]
            together((level, q, place), held)
            held = (level, q, place) if level <= STEPS else None
            if level == STEPS + 1:
                for s in range(2):
                    plane = planes - 1 - q if s else q
                    sent.append(
                        pltpu.make_async_copy(result.at[q - out_low, s], out.at[0, :, plane], sems.at[len(sent)])
                    )
                    sent[-1].start()
    if held is not None:
        together(None, held)
    for made in sent:
        made.wait()


ANYWHERE = pl.BlockSpec(memory_space=pl.ANY)
CLOSE = pl.BlockSpec(memory_space=pltpu.VMEM)
SCALARS = pl.BlockSpec(memory_space=pltpu.SMEM)


def size(*arrays):
    return sum(math.prod(array.shape) * array.dtype.itemsize for array in arrays)


def pack_first(adjoint_in):
    fields, planes, nth, nr = adjoint_in.shape[1:]
    return pl.pallas_call(
        functools.partial(pack_first_kernel, planes),
        out_shape=jax.ShapeDtypeStruct((1, 2, fields, nth, nr), jnp.float32),
        in_specs=[ANYWHERE],
        out_specs=CLOSE,
        scratch_shapes=[pltpu.SemaphoreType.DMA((2,))],
        compiler_params=pltpu.CompilerParams(vmem_limit_bytes=VMEM_MOST),
        name="pack_first",
    )(adjoint_in)


def pack_rest(adjoint_in, sensor, first, groups):
    fields, planes, nth, nr = adjoint_in.shape[1:]
    depths = sum(groups[1:])
    edges = (STEPS - 1, 2, nth, nr)
    shapes = [(count, 2, fields, nth, nr) for count in groups[1:]] + [edges]
    out_shape = [jax.ShapeDtypeStruct(shape, jnp.float32) for shape in shapes]
    return pl.pallas_call(
        functools.partial(pack_rest_kernel, planes, groups),
        out_shape=out_shape,
        in_specs=[ANYWHERE] * 3,
        out_specs=[ANYWHERE] * len(shapes),
        scratch_shapes=[
            pltpu.VMEM((depths, 2, fields, nth, nr), jnp.float32),
            pltpu.VMEM(edges, jnp.float32),
            pltpu.SemaphoreType.DMA((3 * depths + 2 * STEPS,)),
        ],
        cost_estimate=pl.CostEstimate(flops=0, bytes_accessed=2 * size(*out_shape), transcendentals=0),
        compiler_params=pltpu.CompilerParams(vmem_limit_bytes=VMEM_MOST),
        name="pack_rest",
    )(adjoint_in, sensor, first)


def run_stage(stage, groups, coupling, odd, weights, own, sensor, chunks, halos, carried, out):
    fields, planes, nth, nr = own.shape[1:]
    sides = 2 * fields
    slot = (nr // LANES, sides * (nth + PAD) + PAD, LANES)
    close = [weights, own, sensor, *chunks]
    if stage.first:
        close += halos
    close += [carried[key] for key in stage.taken]
    operands = [coupling, odd, *close] + ([] if stage.first else [out])
    in_specs = [SCALARS] * 2 + [CLOSE] * len(close) + ([] if stage.first else [ANYWHERE])
    given = [jax.ShapeDtypeStruct(slot, jnp.float32)] * len(stage.given)
    low, high = stage.todo[STEPS + 1]
    scratch = [
        pltpu.VMEM((high - low, 2, fields, nth, nr), jnp.float32),
        pltpu.VMEM(weights.shape, weights.dtype),
        *[pltpu.VMEM(slot, jnp.float32)] * len(stage.kept),
        *[pltpu.VMEM((sides * nth, nr), jnp.bfloat16)] * 4,
    ]
    limit = VMEM_SPARE + size(*scratch, *close, *given)
    out, *fresh = pl.pallas_call(
        functools.partial(stage_kernel, stage, fields, planes, groups),
        out_shape=[jax.ShapeDtypeStruct(own.shape, jnp.float32), *given],
        in_specs=in_specs,
        out_specs=[ANYWHERE] + [CLOSE] * len(given),
        scratch_shapes=scratch + [pltpu.SemaphoreType.DMA((2 * max(high - low, 1),))],
        input_output_aliases={} if stage.first else {len(operands) - 1: 0},
        cost_estimate=pl.CostEstimate(
            flops=0, bytes_accessed=size(*close, *given) if stage.first else 0, transcendentals=0
        ),
        compiler_params=pltpu.CompilerParams(vmem_limit_bytes=limit),
        name=f"stage_{'first' if stage.first else 'last' if stage.last else 'middle'}",
    )(*operands)
    return out, dict(zip(stage.given, fresh))


def shards(adjoint_in, sensor, filter_matrix, coupling):
    fields, planes, nth, nr = adjoint_in.shape[1:]
    half = planes // 2
    segs = lax.axis_size("seg")
    slabs = lax.axis_size("gx")
    back = [((i + 1) % segs, i) for i in range(segs)]

    groups = []
    for count in GROUPS:
        if sum(groups) + count < half:
            groups.append(count)
    groups.append(half - sum(groups))

    first_chunk = pack_first(adjoint_in)
    *rest, sensor_edges = pack_rest(adjoint_in, sensor, first_chunk, groups)

    odd = lax.rem(lax.axis_index("gx"), 2)

    def swapped(edges):
        result = []
        for parity in range(2):
            pairs = [(i, i + 1) for i in range(parity, slabs - 1, 2)]
            side = 1 - odd if parity == 0 else odd
            mine = jnp.concatenate([lax.dynamic_index_in_dim(part, side, 0, keepdims=False) for part in edges])
            result.append(lax.ppermute(mine, "gx", pairs + [(j, i) for i, j in pairs]))
        return result

    high = lax.reduce_precision(filter_matrix, 8, 7)
    low = filter_matrix - high
    weights = jnp.concatenate([high, high, low], axis=0).astype(jnp.bfloat16)
    scalar = jnp.stack([odd, 0 * odd]).astype(jnp.int32)

    stages = [(0, STEPS)]
    while stages[-1][1] < len(groups):
        low_cut = stages[-1][1]
        stages.append((low_cut, max(min(low_cut + TOGETHER, len(groups) - 1), low_cut + 1)))
    cuts = [sum(groups[:i]) for i in range(len(groups) + 1)]
    carried, out = {}, None
    halos = []

    def run(number):
        nonlocal out
        low_cut, high_cut = stages[number]
        mine = groups[low_cut:high_cut]
        stage = Stage(cuts[low_cut] if number else -STEPS, cuts[high_cut], half)
        out, fresh = run_stage(
            stage, mine, coupling, scalar, weights, adjoint_in, sensor,
            chunks[low_cut:high_cut], halos, carried, out,
        )
        carried.update(fresh)

    chunks, exchanged = [], []
    ran = 0

    def unpack():
        nonlocal halos
        halos = sum(exchanged, [])

    for i, packed in enumerate([first_chunk, *rest]):
        if i >= STEPS + 3 and stages[ran][1] < i:
            if ran == 0:
                unpack()
            run(ran)
            ran += 1
            key = max(carried)
            packed, carried[key] = lax.optimization_barrier((packed, carried[key]))
        elif i > 1:
            k = {STEPS: 0, STEPS + 2: 1}.get(i)
            ends = [] if k is None else exchanged[k]
            packed, weights, chunks[i - 2], *ends = lax.optimization_barrier((packed, weights, chunks[i - 2], *ends))
            if ends:
                exchanged[k] = ends
        chunks.append(lax.ppermute(packed, "seg", back))
        if 1 <= i <= STEPS:
            edges = [chunks[i - 1][0]] + ([sensor_edges[i - 1][:, None]] if i < STEPS else [])
            exchanged.append(swapped(edges))
    for number in range(ran, len(stages)):
        if number == 0:
            unpack()
        run(number)
    return out


def solution(mesh):
    in_specs = (P("seg", None, "gx", None, None), P("seg", "gx", None, None), P(), P())
    out_specs = P("seg", None, "gx", None, None)
    return jax.shard_map(shards, mesh=mesh, in_specs=in_specs, out_specs=out_specs, check_vma=False)
```

```python
import functools
import math

import jax
import jax.numpy as jnp
from jax import lax
from jax.experimental import pallas as pl
from jax.experimental.pallas import tpu as pltpu
from jax.sharding import PartitionSpec as P

STEPS = 3
LANES = 128
PAD = 8
LATE = 1
ROWS = 16
GROUPS = (1, 1, 1, 1, 1, 1, 1)
TOGETHER = 2
VMEM_SPARE = 6 * 1024 * 1024
VMEM_MOST = 60 * 1024 * 1024


class Stage:
    def __init__(self, region, known, half):
        self.half = half
        self.region, self.known = region, known
        self.halos = region[0] < 0 <= known[0]
        self.todo = {}
        for level in range(1, STEPS + 2):
            done = self.reach(known, level)
            self.todo[level] = [q for q in self.reach(region, level) if q not in done]
        made = [(level, q) for level in range(1, STEPS + 1) for q in self.todo[level]]
        self.needs = {
            (level - 1, other)
            for level in range(2, STEPS + 2)
            for q in self.todo[level]
            for other in range(q - 1, min(q + 2, half))
        }
        self.made = made
        self.taken = sorted(self.needs - set(made))
        self.given, self.kept = [], made

    def reach(self, region, level):
        low, high = region
        return range(low + level - 1, high if high == self.half else high - level + 1)

    def hand_on(self, later):
        wanted = set().union(*(stage.needs for stage in later))
        self.given = [key for key in self.made if key in wanted]
        self.kept = [key for key in self.made if key not in wanted]


def pack_first_kernel(planes, source, result, sems):
    made = []
    for s, plane in enumerate((0, planes - 1)):
        made.append(pltpu.make_async_copy(source.at[0, :, plane], result.at[0, s], sems.at[s]))
        made[-1].start()
    for one in made:
        one.wait()


def pack_rest_kernel(planes, groups, source, sensor, first, *refs):
    del first
    *results, held, edges, sems = refs
    plan = []
    depth = groups[0]
    for result, count in zip(results, groups[1:]):
        for k in range(count):
            place = held.at[depth - groups[0] + k]
            plan.append(
                ([(source.at[0, :, depth + k], place.at[0]), (source.at[0, :, planes - 1 - depth - k], place.at[1])],
                 place, result.at[k])
            )
        depth += count
    ends = [
        (sensor.at[0, plane], edges.at[k, s])
        for k in range(STEPS - 1)
        for s, plane in enumerate((k, planes - 1 - k))
    ]
    plan.append((ends, edges, results[-1]))
    count = 0

    def start(source, target):
        nonlocal count
        made = pltpu.make_async_copy(source, target, sems.at[count])
        count += 1
        made.start()
        return made

    inward = [[start(*pair) for pair in pairs] for pairs, _, _ in plan]
    outward = []
    for made, (_, place, result) in zip(inward, plan):
        for one in made:
            one.wait()
        outward.append(start(place, result))
    for one in outward:
        one.wait()


def stage_kernel(stage, fields, planes, aliased, groups, *refs):
    refs = list(refs)

    def take(count):
        got = refs[:count]
        del refs[:count]
        return got

    (coupling, odd_ref, weights_in, sensor) = take(4)
    chunks = take(len(groups))
    halos = take(2 * STEPS) if stage.halos else []
    filtered = dict(zip(stage.taken, take(len(stage.taken))))
    outs = stage.todo[STEPS + 1]
    (own,) = take(1) if outs else [None]
    take(1 if aliased else 0)
    (out,) = take(1) if outs else [None]
    fresh = dict(zip(stage.given, take(len(stage.given))))
    (result, weights) = take(2)
    fresh.update(zip(stage.kept, take(len(stage.kept))))
    filtered.update(fresh)
    highs = take(2)
    lows = take(2)
    (sems,) = take(1)

    sides = 2 * fields
    nth, nr = sensor.shape[-2:]
    blocks = nr // LANES
    stride = nth + PAD
    odd, base = odd_ref[0], odd_ref[1]

    blank = jnp.zeros((PAD, LANES), jnp.float32)
    for ref in fresh.values():

        def clear(i, ref=ref):
            for b in range(blocks):
                ref[b, pl.ds(pl.multiple_of(i * stride, PAD), PAD)] = blank

        pl.loop(0, sides + 1)(clear)

    step = 4 * ROWS

    def fetch(i):
        at = pl.ds(pl.multiple_of(i * step, step), step)
        weights[at] = weights_in[at]

    pl.loop(0, weights.shape[0] // step)(fetch)

    lane = lax.broadcasted_iota(jnp.int32, (ROWS, LANES), 1)
    at_start = lane == 0
    at_end = lane == LANES - 1
    weight = [[coupling[g, f] for f in range(fields)] for g in range(fields)]

    def columns(b):
        return slice(b * LANES, (b + 1) * LANES)

    waiting = []

    def store_late(stores=None):
        if stores is not None:
            waiting.append(stores)
        while len(waiting) > (LATE if stores is not None else 0):
            for store in waiting.pop(0):
                store()

    def put(value, place, row, b):
        at = (pl.ds(pl.multiple_of(row, ROWS), ROWS), columns(b))
        high = value.astype(jnp.bfloat16)
        highs[place][at] = high
        lows[place][at] = (value - high.astype(jnp.float32)).astype(jnp.bfloat16)

    def keep(value, at):
        result[at] = value

    def split_raw(q, place, t):
        for s in range(2):
            if q < 0:
                source = halos[2 * (-1 - q) + s]
                side = 1 - odd if s == 0 else odd
            else:
                chunk, k = starts[q]
                source, side = chunks[chunk].at[k, s], s
            for f in range(fields):
                stores = []
                for b in range(blocks):
                    value = source[f, pl.ds(t, ROWS), columns(b)]
                    stores.append(functools.partial(put, value, place, (side * fields + f) * nth + t, b))
                store_late(stores)

    def sensor_at(q, s, t, b):
        if q >= 0:
            return sensor[0, planes - 1 - q if s else q, pl.ds(t, ROWS), columns(b)]
        pair = [ref[fields, pl.ds(t, ROWS), columns(b)] for ref in halos[2 * (-1 - q) : 2 * (-q)]]
        return jnp.where(odd == s, pair[1], pair[0])

    def advance(level, q, place, t):
        here = filtered[level - 1, q]
        before = filtered[level - 1, q - 1]
        inner = q < stage.half - 1
        after = filtered[level - 1, q + 1] if inner else here
        for s in range(2):
            rows = [(s * fields + f) * stride + PAD + t for f in range(fields)]
            beyond = rows if inner else [((1 - s) * fields + f) * stride + PAD + t for f in range(fields)]
            aligned = [pl.ds(pl.multiple_of(row, PAD), ROWS) for row in rows]
            beyond = [pl.ds(pl.multiple_of(row, PAD), ROWS) for row in beyond]
            middles = [[here[b, aligned[f]] for b in range(blocks)] for f in range(fields)]
            for b in range(blocks):
                laps = []
                for f in range(fields):
                    middle = middles[f][b]
                    lower = middles[f][b - 1] if b else 0.0
                    upper = middles[f][b + 1] if b + 1 < blocks else 0.0
                    left = pltpu.roll(jnp.where(at_end, lower, middle), 1, 1)
                    right = pltpu.roll(jnp.where(at_start, upper, middle), LANES - 1, 1)
                    axial = before[b, aligned[f]] + after[b, beyond[f]]
                    around = here[b, pl.ds(base + (rows[f] - 1), ROWS)] + here[b, pl.ds(base + (rows[f] + 1), ROWS)]
                    laps.append((axial + around) + (left + right) - 6.0 * middle)
                sens = sensor_at(q, s, t, b)
                stores = []
                for f in range(fields):
                    mixed = weight[0][f] * laps[0]
                    for g in range(1, fields):
                        mixed = mixed + weight[g][f] * laps[g]
                    value = middles[f][b] + sens * mixed
                    if level == STEPS + 1:
                        plane = planes - 1 - q if s else q
                        at = (pl.ds(t, ROWS), columns(b))
                        value = value - own[(0, f, plane, *at)]
                        stores.append(functools.partial(keep, value, (outs.index(q), s, f, *at)))
                    else:
                        stores.append(functools.partial(put, value, place, (s * fields + f) * nth + t, b))
                store_late(stores)

    starts = {}
    depth = stage.known[1]
    for i, count in enumerate(groups):
        for k in range(count):
            starts[depth] = (i, k)
            depth += 1

    parts = nth // ROWS
    width = nr // parts

    def project(level, q, place, j):
        high = highs[place][...]
        left = jnp.concatenate([high, lows[place][...], high], axis=1)
        return jnp.dot(left, weights[:, j * width : (j + 1) * width], preferred_element_type=jnp.float32)

    def hold(level, q, product, j):
        for i in range(sides):
            for b in range(width // LANES):
                at = (j * (width // LANES) + b, slice(i * stride + PAD, (i + 1) * stride))
                filtered[level, q][at] = product[i * nth : (i + 1) * nth, columns(b)]

    def together(task, held):
        for j in range(parts):
            product = None if held is None else project(*held, j)
            if task is not None:
                level, q, place = task
                if level == 1:
                    split_raw(q, place, j * ROWS)
                else:
                    advance(level, q, place, j * ROWS)
                store_late()
            if held is not None:
                hold(held[0], held[1], product, j)

    held = None
    sent = []
    for level in range(1, STEPS + 2):
        for q in stage.todo[level]:
            if held is not None and held[0] == level - 1 and abs(held[1] - q) <= 1:
                together(None, held)
                held = None
            place = 0 if held is None else 1 - held[2]
            together((level, q, place), held)
            held = (level, q, place) if level <= STEPS else None
            if level == STEPS + 1:
                for s in range(2):
                    plane = planes - 1 - q if s else q
                    sent.append(
                        pltpu.make_async_copy(result.at[outs.index(q), s], out.at[0, :, plane], sems.at[len(sent)])
                    )
                    sent[-1].start()
    if held is not None:
        together(None, held)
    for made in sent:
        made.wait()


ANYWHERE = pl.BlockSpec(memory_space=pl.ANY)
CLOSE = pl.BlockSpec(memory_space=pltpu.VMEM)
SCALARS = pl.BlockSpec(memory_space=pltpu.SMEM)


def size(*arrays):
    return sum(math.prod(array.shape) * array.dtype.itemsize for array in arrays)


def pack_first(adjoint_in):
    fields, planes, nth, nr = adjoint_in.shape[1:]
    return pl.pallas_call(
        functools.partial(pack_first_kernel, planes),
        out_shape=jax.ShapeDtypeStruct((1, 2, fields, nth, nr), jnp.float32),
        in_specs=[ANYWHERE],
        out_specs=CLOSE,
        scratch_shapes=[pltpu.SemaphoreType.DMA((2,))],
        compiler_params=pltpu.CompilerParams(vmem_limit_bytes=VMEM_MOST),
        name="pack_first",
    )(adjoint_in)


def pack_rest(adjoint_in, sensor, first, groups):
    fields, planes, nth, nr = adjoint_in.shape[1:]
    depths = sum(groups[1:])
    edges = (STEPS - 1, 2, nth, nr)
    shapes = [(count, 2, fields, nth, nr) for count in groups[1:]] + [edges]
    out_shape = [jax.ShapeDtypeStruct(shape, jnp.float32) for shape in shapes]
    return pl.pallas_call(
        functools.partial(pack_rest_kernel, planes, groups),
        out_shape=out_shape,
        in_specs=[ANYWHERE] * 3,
        out_specs=[ANYWHERE] * len(shapes),
        scratch_shapes=[
            pltpu.VMEM((depths, 2, fields, nth, nr), jnp.float32),
            pltpu.VMEM(edges, jnp.float32),
            pltpu.SemaphoreType.DMA((3 * depths + 2 * STEPS,)),
        ],
        cost_estimate=pl.CostEstimate(flops=0, bytes_accessed=2 * size(*out_shape), transcendentals=0),
        compiler_params=pltpu.CompilerParams(vmem_limit_bytes=VMEM_MOST),
        name="pack_rest",
    )(adjoint_in, sensor, first)


def run_stage(stage, groups, coupling, odd, weights, own, sensor, chunks, halos, carried, out):
    fields, planes, nth, nr = own.shape[1:]
    sides = 2 * fields
    slot = (nr // LANES, sides * (nth + PAD) + PAD, LANES)
    outs = len(stage.todo[STEPS + 1])
    close = [weights, sensor, *chunks]
    if stage.halos:
        close += halos
    close += [carried[key] for key in stage.taken]
    if outs:
        close.append(own)
    aliased = bool(outs) and out is not None
    operands = [coupling, odd, *close] + ([out] if aliased else [])
    in_specs = [SCALARS] * 2 + [CLOSE] * len(close) + ([ANYWHERE] if aliased else [])
    given = [jax.ShapeDtypeStruct(slot, jnp.float32)] * len(stage.given)
    written = [jax.ShapeDtypeStruct(own.shape, jnp.float32)] if outs else []
    scratch = [
        pltpu.VMEM((max(outs, 1), 2, fields, nth, nr), jnp.float32),
        pltpu.VMEM(weights.shape, weights.dtype),
        *[pltpu.VMEM(slot, jnp.float32)] * len(stage.kept),
        *[pltpu.VMEM((sides * nth, nr), jnp.bfloat16)] * 4,
    ]
    limit = VMEM_SPARE + size(*scratch, *close, *given)
    fresh = pl.pallas_call(
        functools.partial(stage_kernel, stage, fields, planes, aliased, groups),
        out_shape=[*written, *given],
        in_specs=in_specs,
        out_specs=[ANYWHERE] * len(written) + [CLOSE] * len(given),
        scratch_shapes=scratch + [pltpu.SemaphoreType.DMA((2 * max(outs, 1),))],
        input_output_aliases={len(operands) - 1: 0} if aliased else {},
        cost_estimate=pl.CostEstimate(flops=0, bytes_accessed=0, transcendentals=0),
        compiler_params=pltpu.CompilerParams(vmem_limit_bytes=limit),
        name="stage_" + "_".join(str(q).replace("-", "m") for q in stage.region),
    )(*operands)
    if outs:
        out, *fresh = fresh
    return out, dict(zip(stage.given, fresh))


def shards(adjoint_in, sensor, filter_matrix, coupling):
    fields, planes, nth, nr = adjoint_in.shape[1:]
    half = planes // 2
    segs = lax.axis_size("seg")
    slabs = lax.axis_size("gx")
    back = [((i + 1) % segs, i) for i in range(segs)]

    groups = []
    for count in GROUPS:
        if sum(groups) + count < half:
            groups.append(count)
    groups.append(half - sum(groups))

    first_chunk = pack_first(adjoint_in)
    *rest, sensor_edges = pack_rest(adjoint_in, sensor, first_chunk, groups)

    odd = lax.rem(lax.axis_index("gx"), 2)

    def swapped(edges):
        result = []
        for parity in range(2):
            pairs = [(i, i + 1) for i in range(parity, slabs - 1, 2)]
            side = 1 - odd if parity == 0 else odd
            mine = jnp.concatenate([lax.dynamic_index_in_dim(part, side, 0, keepdims=False) for part in edges])
            result.append(lax.ppermute(mine, "gx", pairs + [(j, i) for i, j in pairs]))
        return result

    high = lax.reduce_precision(filter_matrix, 8, 7)
    low = filter_matrix - high
    weights = jnp.concatenate([high, high, low], axis=0).astype(jnp.bfloat16)
    scalar = jnp.stack([odd, 0 * odd]).astype(jnp.int32)

    cuts = [sum(groups[:i]) for i in range(len(groups) + 1)]
    regions = [(0, cut) for cut in cuts[STEPS + 1 : STEPS + 3]]
    regions.append((-STEPS, regions[-1][1]))
    while regions[-1][1] < half:
        upto = cuts.index(regions[-1][1])
        upto = max(min(upto + TOGETHER, len(groups) - 1), upto + 1)
        regions.append((-STEPS, cuts[upto]))
    stages = [Stage(new, old, half) for old, new in zip([(0, 0), *regions], regions)]
    for number, stage in enumerate(stages):
        stage.hand_on(stages[number + 1 :])
    carried, out = {}, None
    halos = []

    def run(number):
        nonlocal out
        stage = stages[number]
        at = slice(cuts.index(stage.known[1]), cuts.index(stage.region[1]))
        out, fresh = run_stage(
            stage, groups[at], coupling, scalar, weights, adjoint_in, sensor, chunks[at], halos, carried, out
        )
        carried.update(fresh)

    chunks, exchanged = [], []
    ran = 0

    for i, packed in enumerate([first_chunk, *rest]):
        k = {STEPS: 0, STEPS + 1: 1, STEPS + 3: 2}.get(i)
        ends = exchanged[k] if k is not None and k < len(exchanged) else []
        if i >= STEPS + 3 and not stages[ran].halos and cuts.index(stages[ran].region[1]) < i:
            run(ran)
            key = stages[ran].given[-1]
            ran += 1
            packed, carried[key], *ends = lax.optimization_barrier((packed, carried[key], *ends))
        elif i > 1:
            packed, weights, chunks[i - 2], *ends = lax.optimization_barrier((packed, weights, chunks[i - 2], *ends))
        if ends:
            exchanged[k] = ends
        chunks.append(lax.ppermute(packed, "seg", back))
        if 1 <= i <= STEPS:
            edges = [chunks[i - 1][0]] + ([sensor_edges[i - 1][:, None]] if i < STEPS else [])
            exchanged.append(swapped(edges))
    halos = sum(exchanged, [])
    for number in range(ran, len(stages)):
        run(number)
    return out


def solution(mesh):
    in_specs = (P("seg", None, "gx", None, None), P("seg", "gx", None, None), P(), P())
    out_specs = P("seg", None, "gx", None, None)
    return jax.shard_map(shards, mesh=mesh, in_specs=in_specs, out_specs=out_specs, check_vma=False)
```

```python
import functools
import math

import jax
import jax.numpy as jnp
from jax import lax
from jax.experimental import pallas as pl
from jax.experimental.pallas import tpu as pltpu
from jax.sharding import PartitionSpec as P

STEPS = 3
LANES = 128
PAD = 8
LATE = 1
ROWS = 16
GROUPS = (1, 1, 1, 1, 1, 1, 1)
TOGETHER = 2
VMEM_SPARE = 6 * 1024 * 1024
VMEM_MOST = 60 * 1024 * 1024


class Stage:
    def __init__(self, region, known, half):
        self.half = half
        self.region, self.known = region, known
        self.halos = region[0] < 0 <= known[0]
        self.todo = {}
        for level in range(1, STEPS + 2):
            done = self.reach(known, level)
            self.todo[level] = [q for q in self.reach(region, level) if q not in done]
        made = [(level, q) for level in range(1, STEPS + 1) for q in self.todo[level]]
        self.needs = {
            (level - 1, other)
            for level in range(2, STEPS + 2)
            for q in self.todo[level]
            for other in range(q - 1, min(q + 2, half))
        }
        self.made = made
        self.taken = sorted(self.needs - set(made))
        self.given, self.kept = [], made

    def reach(self, region, level):
        low, high = region
        return range(low + level - 1, high if high == self.half else high - level + 1)

    def hand_on(self, later):
        wanted = set().union(*(stage.needs for stage in later))
        self.given = [key for key in self.made if key in wanted]
        self.kept = [key for key in self.made if key not in wanted]


def pack_first_kernel(planes, source, result, sems):
    made = []
    for s, plane in enumerate((0, planes - 1)):
        made.append(pltpu.make_async_copy(source.at[0, :, plane], result.at[0, s], sems.at[s]))
        made[-1].start()
    for one in made:
        one.wait()


def pack_rest_kernel(planes, groups, source, sensor, first, *refs):
    del first
    *results, held, edges, sems = refs
    plan = []
    depth = groups[0]
    for result, count in zip(results, groups[1:]):
        for k in range(count):
            place = held.at[depth - groups[0] + k]
            plan.append(
                ([(source.at[0, :, depth + k], place.at[0]), (source.at[0, :, planes - 1 - depth - k], place.at[1])],
                 place, result.at[k])
            )
        depth += count
    ends = [
        (sensor.at[0, plane], edges.at[k, s])
        for k in range(STEPS - 1)
        for s, plane in enumerate((k, planes - 1 - k))
    ]
    plan.append((ends, edges, results[-1]))
    count = 0

    def start(source, target):
        nonlocal count
        made = pltpu.make_async_copy(source, target, sems.at[count])
        count += 1
        made.start()
        return made

    inward = [[start(*pair) for pair in pairs] for pairs, _, _ in plan]
    outward = []
    for made, (_, place, result) in zip(inward, plan):
        for one in made:
            one.wait()
        outward.append(start(place, result))
    for one in outward:
        one.wait()


def stage_kernel(stage, fields, planes, aliased, groups, *refs):
    refs = list(refs)

    def take(count):
        got = refs[:count]
        del refs[:count]
        return got

    (coupling, odd_ref, weights, sensor) = take(4)
    chunks = take(len(groups))
    halos = take(2 * STEPS) if stage.halos else []
    filtered = dict(zip(stage.taken, take(len(stage.taken))))
    outs = stage.todo[STEPS + 1]
    (own,) = take(1) if outs else [None]
    take(1 if aliased else 0)
    (out,) = take(1) if outs else [None]
    fresh = dict(zip(stage.given, take(len(stage.given))))
    (result,) = take(1)
    fresh.update(zip(stage.kept, take(len(stage.kept))))
    filtered.update(fresh)
    highs = take(2)
    lows = take(2)
    (sems,) = take(1)

    sides = 2 * fields
    nth, nr = sensor.shape[-2:]
    blocks = nr // LANES
    stride = nth + PAD
    odd, base = odd_ref[0], odd_ref[1]

    blank = jnp.zeros((PAD, LANES), jnp.float32)
    for ref in fresh.values():

        def clear(i, ref=ref):
            for b in range(blocks):
                ref[b, pl.ds(pl.multiple_of(i * stride, PAD), PAD)] = blank

        pl.loop(0, sides + 1)(clear)

    lane = lax.broadcasted_iota(jnp.int32, (ROWS, LANES), 1)
    at_start = lane == 0
    at_end = lane == LANES - 1
    weight = [[coupling[g, f] for f in range(fields)] for g in range(fields)]

    def columns(b):
        return slice(b * LANES, (b + 1) * LANES)

    waiting = []

    def store_late(stores=None):
        if stores is not None:
            waiting.append(stores)
        while len(waiting) > (LATE if stores is not None else 0):
            for store in waiting.pop(0):
                store()

    def put(value, place, row, b):
        at = (pl.ds(pl.multiple_of(row, ROWS), ROWS), columns(b))
        high = value.astype(jnp.bfloat16)
        highs[place][at] = high
        lows[place][at] = (value - high.astype(jnp.float32)).astype(jnp.bfloat16)

    def keep(value, at):
        result[at] = value

    def split_raw(q, place, t):
        for s in range(2):
            if q < 0:
                source = halos[2 * (-1 - q) + s]
                side = 1 - odd if s == 0 else odd
            else:
                chunk, k = starts[q]
                source, side = chunks[chunk].at[k, s], s
            for f in range(fields):
                stores = []
                for b in range(blocks):
                    value = source[f, pl.ds(t, ROWS), columns(b)]
                    stores.append(functools.partial(put, value, place, (side * fields + f) * nth + t, b))
                store_late(stores)

    def sensor_at(q, s, t, b):
        if q >= 0:
            return sensor[0, planes - 1 - q if s else q, pl.ds(t, ROWS), columns(b)]
        pair = [ref[fields, pl.ds(t, ROWS), columns(b)] for ref in halos[2 * (-1 - q) : 2 * (-q)]]
        return jnp.where(odd == s, pair[1], pair[0])

    def advance(level, q, place, t):
        here = filtered[level - 1, q]
        before = filtered[level - 1, q - 1]
        inner = q < stage.half - 1
        after = filtered[level - 1, q + 1] if inner else here
        for s in range(2):
            rows = [(s * fields + f) * stride + PAD + t for f in range(fields)]
            beyond = rows if inner else [((1 - s) * fields + f) * stride + PAD + t for f in range(fields)]
            aligned = [pl.ds(pl.multiple_of(row, PAD), ROWS) for row in rows]
            beyond = [pl.ds(pl.multiple_of(row, PAD), ROWS) for row in beyond]
            middles = [[here[b, aligned[f]] for b in range(blocks)] for f in range(fields)]
            for b in range(blocks):
                laps = []
                for f in range(fields):
                    middle = middles[f][b]
                    lower = middles[f][b - 1] if b else 0.0
                    upper = middles[f][b + 1] if b + 1 < blocks else 0.0
                    left = pltpu.roll(jnp.where(at_end, lower, middle), 1, 1)
                    right = pltpu.roll(jnp.where(at_start, upper, middle), LANES - 1, 1)
                    axial = before[b, aligned[f]] + after[b, beyond[f]]
                    around = here[b, pl.ds(base + (rows[f] - 1), ROWS)] + here[b, pl.ds(base + (rows[f] + 1), ROWS)]
                    laps.append((axial + around) + (left + right) - 6.0 * middle)
                sens = sensor_at(q, s, t, b)
                stores = []
                for f in range(fields):
                    mixed = weight[0][f] * laps[0]
                    for g in range(1, fields):
                        mixed = mixed + weight[g][f] * laps[g]
                    value = middles[f][b] + sens * mixed
                    if level == STEPS + 1:
                        plane = planes - 1 - q if s else q
                        at = (pl.ds(t, ROWS), columns(b))
                        value = value - own[(0, f, plane, *at)]
                        stores.append(functools.partial(keep, value, (outs.index(q), s, f, *at)))
                    else:
                        stores.append(functools.partial(put, value, place, (s * fields + f) * nth + t, b))
                store_late(stores)

    starts = {}
    depth = stage.known[1]
    for i, count in enumerate(groups):
        for k in range(count):
            starts[depth] = (i, k)
            depth += 1

    parts = nth // ROWS
    width = nr // parts

    def project(level, q, place, j):
        high = highs[place][...]
        left = jnp.concatenate([high, lows[place][...], high], axis=1)
        return jnp.dot(left, weights[:, j * width : (j + 1) * width], preferred_element_type=jnp.float32)

    def hold(level, q, product, j):
        for i in range(sides):
            for b in range(width // LANES):
                at = (j * (width // LANES) + b, slice(i * stride + PAD, (i + 1) * stride))
                filtered[level, q][at] = product[i * nth : (i + 1) * nth, columns(b)]

    def together(task, held):
        for j in range(parts):
            product = None if held is None else project(*held, j)
            if task is not None:
                level, q, place = task
                if level == 1:
                    split_raw(q, place, j * ROWS)
                else:
                    advance(level, q, place, j * ROWS)
                store_late()
            if held is not None:
                hold(held[0], held[1], product, j)

    held = None
    sent = []
    for level in range(1, STEPS + 2):
        for q in stage.todo[level]:
            if held is not None and held[0] == level - 1 and abs(held[1] - q) <= 1:
                together(None, held)
                held = None
            place = 0 if held is None else 1 - held[2]
            together((level, q, place), held)
            held = (level, q, place) if level <= STEPS else None
            if level == STEPS + 1:
                for s in range(2):
                    plane = planes - 1 - q if s else q
                    sent.append(
                        pltpu.make_async_copy(result.at[outs.index(q), s], out.at[0, :, plane], sems.at[len(sent)])
                    )
                    sent[-1].start()
    if held is not None:
        together(None, held)
    for made in sent:
        made.wait()


ANYWHERE = pl.BlockSpec(memory_space=pl.ANY)
CLOSE = pl.BlockSpec(memory_space=pltpu.VMEM)
SCALARS = pl.BlockSpec(memory_space=pltpu.SMEM)


def size(*arrays):
    return sum(math.prod(array.shape) * array.dtype.itemsize for array in arrays)


def pack_first(adjoint_in):
    fields, planes, nth, nr = adjoint_in.shape[1:]
    return pl.pallas_call(
        functools.partial(pack_first_kernel, planes),
        out_shape=jax.ShapeDtypeStruct((1, 2, fields, nth, nr), jnp.float32),
        in_specs=[ANYWHERE],
        out_specs=CLOSE,
        scratch_shapes=[pltpu.SemaphoreType.DMA((2,))],
        compiler_params=pltpu.CompilerParams(vmem_limit_bytes=VMEM_MOST),
        name="pack_first",
    )(adjoint_in)


def pack_rest(adjoint_in, sensor, first, groups):
    fields, planes, nth, nr = adjoint_in.shape[1:]
    depths = sum(groups[1:])
    edges = (STEPS - 1, 2, nth, nr)
    shapes = [(count, 2, fields, nth, nr) for count in groups[1:]] + [edges]
    out_shape = [jax.ShapeDtypeStruct(shape, jnp.float32) for shape in shapes]
    return pl.pallas_call(
        functools.partial(pack_rest_kernel, planes, groups),
        out_shape=out_shape,
        in_specs=[ANYWHERE] * 3,
        out_specs=[ANYWHERE] * len(shapes),
        scratch_shapes=[
            pltpu.VMEM((depths, 2, fields, nth, nr), jnp.float32),
            pltpu.VMEM(edges, jnp.float32),
            pltpu.SemaphoreType.DMA((3 * depths + 2 * STEPS,)),
        ],
        cost_estimate=pl.CostEstimate(flops=0, bytes_accessed=2 * size(*out_shape), transcendentals=0),
        compiler_params=pltpu.CompilerParams(vmem_limit_bytes=VMEM_MOST),
        name="pack_rest",
    )(adjoint_in, sensor, first)


def run_stage(stage, groups, coupling, odd, weights, own, sensor, chunks, halos, carried, out):
    fields, planes, nth, nr = own.shape[1:]
    sides = 2 * fields
    slot = (nr // LANES, sides * (nth + PAD) + PAD, LANES)
    outs = len(stage.todo[STEPS + 1])
    close = [weights, sensor, *chunks]
    if stage.halos:
        close += halos
    close += [carried[key] for key in stage.taken]
    if outs:
        close.append(own)
    aliased = bool(outs) and out is not None
    operands = [coupling, odd, *close] + ([out] if aliased else [])
    in_specs = [SCALARS] * 2 + [CLOSE] * len(close) + ([ANYWHERE] if aliased else [])
    given = [jax.ShapeDtypeStruct(slot, jnp.float32)] * len(stage.given)
    written = [jax.ShapeDtypeStruct(own.shape, jnp.float32)] if outs else []
    scratch = [
        pltpu.VMEM((max(outs, 1), 2, fields, nth, nr), jnp.float32),
        *[pltpu.VMEM(slot, jnp.float32)] * len(stage.kept),
        *[pltpu.VMEM((sides * nth, nr), jnp.bfloat16)] * 4,
    ]
    limit = VMEM_SPARE + size(*scratch, *close, *given)
    fresh = pl.pallas_call(
        functools.partial(stage_kernel, stage, fields, planes, aliased, groups),
        out_shape=[*written, *given],
        in_specs=in_specs,
        out_specs=[ANYWHERE] * len(written) + [CLOSE] * len(given),
        scratch_shapes=scratch + [pltpu.SemaphoreType.DMA((2 * max(outs, 1),))],
        input_output_aliases={len(operands) - 1: 0} if aliased else {},
        cost_estimate=pl.CostEstimate(flops=0, bytes_accessed=0, transcendentals=0),
        compiler_params=pltpu.CompilerParams(vmem_limit_bytes=limit),
        name="stage_" + "_".join(str(q).replace("-", "m") for q in stage.region),
    )(*operands)
    if outs:
        out, *fresh = fresh
    return out, dict(zip(stage.given, fresh))


def shards(adjoint_in, sensor, filter_matrix, coupling):
    fields, planes, nth, nr = adjoint_in.shape[1:]
    half = planes // 2
    segs = lax.axis_size("seg")
    slabs = lax.axis_size("gx")
    back = [((i + 1) % segs, i) for i in range(segs)]

    groups = []
    for count in GROUPS:
        if sum(groups) + count < half:
            groups.append(count)
    groups.append(half - sum(groups))

    first_chunk = pack_first(adjoint_in)
    *rest, sensor_edges = pack_rest(adjoint_in, sensor, first_chunk, groups)

    odd = lax.rem(lax.axis_index("gx"), 2)

    def swapped(edges, after=None):
        result = []
        for parity in range(2):
            pairs = [(i, i + 1) for i in range(parity, slabs - 1, 2)]
            side = 1 - odd if parity == 0 else odd
            if parity and after is not None:
                chunks[after], *edges = lax.optimization_barrier((chunks[after], *edges))
            mine = jnp.concatenate([lax.dynamic_index_in_dim(part, side, 0, keepdims=False) for part in edges])
            result.append(lax.ppermute(mine, "gx", pairs + [(j, i) for i, j in pairs]))
        return result

    high = lax.reduce_precision(filter_matrix, 8, 7)
    low = filter_matrix - high
    weights = jnp.concatenate([high, high, low], axis=0).astype(jnp.bfloat16)
    scalar = jnp.stack([odd, 0 * odd]).astype(jnp.int32)

    cuts = [sum(groups[:i]) for i in range(len(groups) + 1)]
    regions = [(0, cut) for cut in cuts[STEPS + 1 : STEPS + 3]]
    regions.append((-STEPS, regions[-1][1]))
    while regions[-1][1] < half:
        upto = cuts.index(regions[-1][1])
        upto = max(min(upto + TOGETHER, len(groups) - 1), upto + 1)
        regions.append((-STEPS, cuts[upto]))
    stages = [Stage(new, old, half) for old, new in zip([(0, 0), *regions], regions)]
    for number, stage in enumerate(stages):
        stage.hand_on(stages[number + 1 :])
    carried, out = {}, None
    halos = []

    def run(number):
        nonlocal out
        stage = stages[number]
        at = slice(cuts.index(stage.known[1]), cuts.index(stage.region[1]))
        out, fresh = run_stage(
            stage, groups[at], coupling, scalar, weights, adjoint_in, sensor, chunks[at], halos, carried, out
        )
        carried.update(fresh)

    chunks, exchanged = [], []
    ran = 0

    for i, packed in enumerate([first_chunk, *rest]):
        k = {STEPS: 0, STEPS + 1: 1, STEPS + 3: 2}.get(i)
        ends = exchanged[k] if k is not None and k < len(exchanged) else []
        if i >= STEPS + 3 and not stages[ran].halos and cuts.index(stages[ran].region[1]) < i:
            run(ran)
            key = stages[ran].given[-1]
            ran += 1
            packed, carried[key], *ends = lax.optimization_barrier((packed, carried[key], *ends))
        elif i > 1:
            packed, weights, chunks[i - 2], *ends = lax.optimization_barrier((packed, weights, chunks[i - 2], *ends))
        if ends:
            exchanged[k] = ends
        chunks.append(lax.ppermute(packed, "seg", back))
        if 1 <= i <= STEPS:
            edges = [chunks[i - 1][0]] + ([sensor_edges[i - 1][:, None]] if i < STEPS else [])
            exchanged.append(swapped(edges, i if i == STEPS else None))
    halos = sum(exchanged, [])
    for number in range(ran, len(stages)):
        run(number)
    return out


def solution(mesh):
    in_specs = (P("seg", None, "gx", None, None), P("seg", "gx", None, None), P(), P())
    out_specs = P("seg", None, "gx", None, None)
    return jax.shard_map(shards, mesh=mesh, in_specs=in_specs, out_specs=out_specs, check_vma=False)
```

```python
import functools
import math

import jax
import jax.numpy as jnp
from jax import lax
from jax.experimental import pallas as pl
from jax.experimental.pallas import tpu as pltpu
from jax.sharding import PartitionSpec as P

STEPS = 3
LANES = 128
PAD = 8
LATE = 1
ROWS = 16
GROUPS = (1, 1, 1, 1, 1, 1, 1)
TOGETHER = 2
VMEM_SPARE = 6 * 1024 * 1024
VMEM_MOST = 60 * 1024 * 1024


class Stage:
    def __init__(self, region, known, half):
        self.half = half
        self.region, self.known = region, known
        self.halos = region[0] < 0 <= known[0]
        self.todo = {}
        for level in range(1, STEPS + 2):
            done = self.reach(known, level)
            self.todo[level] = [q for q in self.reach(region, level) if q not in done]
        made = [(level, q) for level in range(1, STEPS + 1) for q in self.todo[level]]
        self.needs = {
            (level - 1, other)
            for level in range(2, STEPS + 2)
            for q in self.todo[level]
            for other in range(q - 1, min(q + 2, half))
        }
        self.made = made
        self.taken = sorted(self.needs - set(made))
        self.given, self.kept = [], made

    def reach(self, region, level):
        low, high = region
        return range(low + level - 1, high if high == self.half else high - level + 1)

    def hand_on(self, later):
        wanted = set().union(*(stage.needs for stage in later))
        self.given = [key for key in self.made if key in wanted]
        self.kept = [key for key in self.made if key not in wanted]


def pack_first_kernel(planes, source, result, sems):
    made = []
    for s, plane in enumerate((0, planes - 1)):
        made.append(pltpu.make_async_copy(source.at[0, :, plane], result.at[0, s], sems.at[s]))
        made[-1].start()
    for one in made:
        one.wait()


def pack_rest_kernel(planes, groups, source, sensor, first, *refs):
    del first
    *results, held, edges, sems = refs
    plan = []
    depth = groups[0]
    for result, count in zip(results, groups[1:]):
        for k in range(count):
            place = held.at[depth - groups[0] + k]
            plan.append(
                ([(source.at[0, :, depth + k], place.at[0]), (source.at[0, :, planes - 1 - depth - k], place.at[1])],
                 place, result.at[k])
            )
        depth += count
    ends = [
        (sensor.at[0, plane], edges.at[k, s])
        for k in range(STEPS - 1)
        for s, plane in enumerate((k, planes - 1 - k))
    ]
    plan.append((ends, edges, results[-1]))
    count = 0

    def start(source, target):
        nonlocal count
        made = pltpu.make_async_copy(source, target, sems.at[count])
        count += 1
        made.start()
        return made

    inward = [[start(*pair) for pair in pairs] for pairs, _, _ in plan]
    outward = []
    for made, (_, place, result) in zip(inward, plan):
        for one in made:
            one.wait()
        outward.append(start(place, result))
    for one in outward:
        one.wait()


def stage_kernel(stage, fields, planes, aliased, groups, *refs):
    refs = list(refs)

    def take(count):
        got = refs[:count]
        del refs[:count]
        return got

    (coupling, odd_ref, weights, sensor) = take(4)
    chunks = take(len(groups))
    halos = take(2 * STEPS) if stage.halos else []
    filtered = dict(zip(stage.taken, take(len(stage.taken))))
    outs = stage.todo[STEPS + 1]
    (own,) = take(1) if outs else [None]
    take(1 if aliased else 0)
    (out,) = take(1) if outs else [None]
    fresh = dict(zip(stage.given, take(len(stage.given))))
    (result,) = take(1)
    fresh.update(zip(stage.kept, take(len(stage.kept))))
    filtered.update(fresh)
    highs = take(2)
    lows = take(2)
    (sems,) = take(1)

    sides = 2 * fields
    nth, nr = sensor.shape[-2:]
    blocks = nr // LANES
    stride = nth + PAD
    odd, base = odd_ref[0], odd_ref[1]

    blank = jnp.zeros((PAD, LANES), jnp.float32)
    for ref in fresh.values():

        def clear(i, ref=ref):
            for b in range(blocks):
                ref[b, pl.ds(pl.multiple_of(i * stride, PAD), PAD)] = blank

        pl.loop(0, sides + 1)(clear)

    lane = lax.broadcasted_iota(jnp.int32, (ROWS, LANES), 1)
    at_start = lane == 0
    at_end = lane == LANES - 1
    weight = [[coupling[g, f] for f in range(fields)] for g in range(fields)]

    def columns(b):
        return slice(b * LANES, (b + 1) * LANES)

    waiting = []

    def store_late(stores=None):
        if stores is not None:
            waiting.append(stores)
        while len(waiting) > (LATE if stores is not None else 0):
            for store in waiting.pop(0):
                store()

    def put(value, place, row, b):
        at = (pl.ds(pl.multiple_of(row, ROWS), ROWS), columns(b))
        high = value.astype(jnp.bfloat16)
        highs[place][at] = high
        lows[place][at] = (value - high.astype(jnp.float32)).astype(jnp.bfloat16)

    def keep(value, at):
        result[at] = value

    def split_raw(q, place, t):
        for s in range(2):
            if q < 0:
                source = halos[2 * (-1 - q) + s]
                side = 1 - odd if s == 0 else odd
            else:
                chunk, k = starts[q]
                source, side = chunks[chunk].at[k, s], s
            for f in range(fields):
                stores = []
                for b in range(blocks):
                    value = source[f, pl.ds(t, ROWS), columns(b)]
                    stores.append(functools.partial(put, value, place, (side * fields + f) * nth + t, b))
                store_late(stores)

    def sensor_at(q, s, t, b):
        if q >= 0:
            return sensor[0, planes - 1 - q if s else q, pl.ds(t, ROWS), columns(b)]
        pair = [ref[fields, pl.ds(t, ROWS), columns(b)] for ref in halos[2 * (-1 - q) : 2 * (-q)]]
        return jnp.where(odd == s, pair[1], pair[0])

    def advance(level, q, place, t):
        here = filtered[level - 1, q]
        before = filtered[level - 1, q - 1]
        inner = q < stage.half - 1
        after = filtered[level - 1, q + 1] if inner else here
        for s in range(2):
            rows = [(s * fields + f) * stride + PAD + t for f in range(fields)]
            beyond = rows if inner else [((1 - s) * fields + f) * stride + PAD + t for f in range(fields)]
            aligned = [pl.ds(pl.multiple_of(row, PAD), ROWS) for row in rows]
            beyond = [pl.ds(pl.multiple_of(row, PAD), ROWS) for row in beyond]
            middles = [[here[b, aligned[f]] for b in range(blocks)] for f in range(fields)]
            for b in range(blocks):
                laps = []
                for f in range(fields):
                    middle = middles[f][b]
                    lower = middles[f][b - 1] if b else 0.0
                    upper = middles[f][b + 1] if b + 1 < blocks else 0.0
                    left = pltpu.roll(jnp.where(at_end, lower, middle), 1, 1)
                    right = pltpu.roll(jnp.where(at_start, upper, middle), LANES - 1, 1)
                    axial = before[b, aligned[f]] + after[b, beyond[f]]
                    around = here[b, pl.ds(base + (rows[f] - 1), ROWS)] + here[b, pl.ds(base + (rows[f] + 1), ROWS)]
                    laps.append((axial + around) + (left + right) - 6.0 * middle)
                sens = sensor_at(q, s, t, b)
                stores = []
                for f in range(fields):
                    mixed = weight[0][f] * laps[0]
                    for g in range(1, fields):
                        mixed = mixed + weight[g][f] * laps[g]
                    value = middles[f][b] + sens * mixed
                    if level == STEPS + 1:
                        plane = planes - 1 - q if s else q
                        at = (pl.ds(t, ROWS), columns(b))
                        value = value - own[(0, f, plane, *at)]
                        stores.append(functools.partial(keep, value, (outs.index(q), s, f, *at)))
                    else:
                        stores.append(functools.partial(put, value, place, (s * fields + f) * nth + t, b))
                store_late(stores)

    starts = {}
    depth = stage.known[1]
    for i, count in enumerate(groups):
        for k in range(count):
            starts[depth] = (i, k)
            depth += 1

    parts = nth // ROWS
    width = nr // parts

    def project(level, q, place, j):
        high = highs[place][...]
        left = jnp.concatenate([high, lows[place][...], high], axis=1)
        return jnp.dot(left, weights[:, j * width : (j + 1) * width], preferred_element_type=jnp.float32)

    def hold(level, q, product, j):
        for i in range(sides):
            for b in range(width // LANES):
                at = (j * (width // LANES) + b, slice(i * stride + PAD, (i + 1) * stride))
                filtered[level, q][at] = product[i * nth : (i + 1) * nth, columns(b)]

    def together(task, held):
        for j in range(parts):
            product = None if held is None else project(*held, j)
            if task is not None:
                level, q, place = task
                if level == 1:
                    split_raw(q, place, j * ROWS)
                else:
                    advance(level, q, place, j * ROWS)
                store_late()
            if held is not None:
                hold(held[0], held[1], product, j)

    held = None
    sent = []
    for level in range(1, STEPS + 2):
        for q in stage.todo[level]:
            if held is not None and held[0] == level - 1 and abs(held[1] - q) <= 1:
                together(None, held)
                held = None
            place = 0 if held is None else 1 - held[2]
            together((level, q, place), held)
            held = (level, q, place) if level <= STEPS else None
            if level == STEPS + 1:
                for s in range(2):
                    plane = planes - 1 - q if s else q
                    sent.append(
                        pltpu.make_async_copy(result.at[outs.index(q), s], out.at[0, :, plane], sems.at[len(sent)])
                    )
                    sent[-1].start()
    if held is not None:
        together(None, held)
    for made in sent:
        made.wait()


ANYWHERE = pl.BlockSpec(memory_space=pl.ANY)
CLOSE = pl.BlockSpec(memory_space=pltpu.VMEM)
SCALARS = pl.BlockSpec(memory_space=pltpu.SMEM)


def size(*arrays):
    return sum(math.prod(array.shape) * array.dtype.itemsize for array in arrays)


def pack_first(adjoint_in):
    fields, planes, nth, nr = adjoint_in.shape[1:]
    return pl.pallas_call(
        functools.partial(pack_first_kernel, planes),
        out_shape=jax.ShapeDtypeStruct((1, 2, fields, nth, nr), jnp.float32),
        in_specs=[ANYWHERE],
        out_specs=CLOSE,
        scratch_shapes=[pltpu.SemaphoreType.DMA((2,))],
        compiler_params=pltpu.CompilerParams(vmem_limit_bytes=VMEM_MOST),
        name="pack_first",
    )(adjoint_in)


def pack_rest(adjoint_in, sensor, first, groups):
    fields, planes, nth, nr = adjoint_in.shape[1:]
    depths = sum(groups[1:])
    edges = (STEPS - 1, 2, nth, nr)
    shapes = [(count, 2, fields, nth, nr) for count in groups[1:]] + [edges]
    out_shape = [jax.ShapeDtypeStruct(shape, jnp.float32) for shape in shapes]
    return pl.pallas_call(
        functools.partial(pack_rest_kernel, planes, groups),
        out_shape=out_shape,
        in_specs=[ANYWHERE] * 3,
        out_specs=[ANYWHERE] * len(shapes),
        scratch_shapes=[
            pltpu.VMEM((depths, 2, fields, nth, nr), jnp.float32),
            pltpu.VMEM(edges, jnp.float32),
            pltpu.SemaphoreType.DMA((3 * depths + 2 * STEPS,)),
        ],
        cost_estimate=pl.CostEstimate(flops=0, bytes_accessed=2 * size(*out_shape), transcendentals=0),
        compiler_params=pltpu.CompilerParams(vmem_limit_bytes=VMEM_MOST),
        name="pack_rest",
    )(adjoint_in, sensor, first)


def run_stage(stage, groups, coupling, odd, weights, own, sensor, chunks, halos, carried, out):
    fields, planes, nth, nr = own.shape[1:]
    sides = 2 * fields
    slot = (nr // LANES, sides * (nth + PAD) + PAD, LANES)
    outs = len(stage.todo[STEPS + 1])
    close = [weights, sensor, *chunks]
    if stage.halos:
        close += halos
    close += [carried[key] for key in stage.taken]
    if outs:
        close.append(own)
    aliased = bool(outs) and out is not None
    operands = [coupling, odd, *close] + ([out] if aliased else [])
    in_specs = [SCALARS] * 2 + [CLOSE] * len(close) + ([ANYWHERE] if aliased else [])
    given = [jax.ShapeDtypeStruct(slot, jnp.float32)] * len(stage.given)
    written = [jax.ShapeDtypeStruct(own.shape, jnp.float32)] if outs else []
    scratch = [
        pltpu.VMEM((max(outs, 1), 2, fields, nth, nr), jnp.float32),
        *[pltpu.VMEM(slot, jnp.float32)] * len(stage.kept),
        *[pltpu.VMEM((sides * nth, nr), jnp.bfloat16)] * 4,
    ]
    limit = VMEM_SPARE + size(*scratch, *close, *given)
    fresh = pl.pallas_call(
        functools.partial(stage_kernel, stage, fields, planes, aliased, groups),
        out_shape=[*written, *given],
        in_specs=in_specs,
        out_specs=[ANYWHERE] * len(written) + [CLOSE] * len(given),
        scratch_shapes=scratch + [pltpu.SemaphoreType.DMA((2 * max(outs, 1),))],
        input_output_aliases={len(operands) - 1: 0} if aliased else {},
        cost_estimate=pl.CostEstimate(flops=0, bytes_accessed=0, transcendentals=0),
        compiler_params=pltpu.CompilerParams(vmem_limit_bytes=limit),
        name="stage_" + "_".join(str(q).replace("-", "m") for q in stage.region),
    )(*operands)
    if outs:
        out, *fresh = fresh
    return out, dict(zip(stage.given, fresh))


def shards(adjoint_in, sensor, filter_matrix, coupling):
    fields, planes, nth, nr = adjoint_in.shape[1:]
    half = planes // 2
    segs = lax.axis_size("seg")
    slabs = lax.axis_size("gx")
    back = [((i + 1) % segs, i) for i in range(segs)]

    groups = []
    for count in GROUPS:
        if sum(groups) + count < half:
            groups.append(count)
    groups.append(half - sum(groups))

    first_chunk = pack_first(adjoint_in)
    *rest, sensor_edges = pack_rest(adjoint_in, sensor, first_chunk, groups)

    odd = lax.rem(lax.axis_index("gx"), 2)

    def swapped(edges, parities=(0, 1)):
        result = []
        for parity in parities:
            pairs = [(i, i + 1) for i in range(parity, slabs - 1, 2)]
            side = 1 - odd if parity == 0 else odd
            mine = jnp.concatenate([lax.dynamic_index_in_dim(part, side, 0, keepdims=False) for part in edges])
            result.append(lax.ppermute(mine, "gx", pairs + [(j, i) for i, j in pairs]))
        return result

    high = lax.reduce_precision(filter_matrix, 8, 7)
    low = filter_matrix - high
    weights = jnp.concatenate([high, high, low], axis=0).astype(jnp.bfloat16)
    scalar = jnp.stack([odd, 0 * odd]).astype(jnp.int32)

    cuts = [sum(groups[:i]) for i in range(len(groups) + 1)]
    regions = [(0, cut) for cut in cuts[STEPS + 1 : STEPS + 3]]
    regions.append((-STEPS, regions[-1][1]))
    while regions[-1][1] < half:
        upto = cuts.index(regions[-1][1])
        upto = max(min(upto + TOGETHER, len(groups) - 1), upto + 1)
        regions.append((-STEPS, cuts[upto]))
    stages = [Stage(new, old, half) for old, new in zip([(0, 0), *regions], regions)]
    for number, stage in enumerate(stages):
        stage.hand_on(stages[number + 1 :])
    carried, out = {}, None
    halos = []

    def run(number):
        nonlocal out
        stage = stages[number]
        at = slice(cuts.index(stage.known[1]), cuts.index(stage.region[1]))
        out, fresh = run_stage(
            stage, groups[at], coupling, scalar, weights, adjoint_in, sensor, chunks[at], halos, carried, out
        )
        carried.update(fresh)

    chunks, exchanged = [], []
    ran = 0

    for i, packed in enumerate([first_chunk, *rest]):
        k = {STEPS: 0, STEPS + 1: 1, STEPS + 3: 2}.get(i)
        ends = exchanged[k] if k is not None and k < len(exchanged) else []
        if i >= STEPS + 3 and not stages[ran].halos and cuts.index(stages[ran].region[1]) < i:
            run(ran)
            key = stages[ran].given[-1]
            ran += 1
            if k is not None:
                edge, carried[key] = lax.optimization_barrier((chunks[STEPS - 1][0], carried[key]))
                ends = swapped([edge], (0,)) + ends
            packed, carried[key], *ends = lax.optimization_barrier((packed, carried[key], *ends))
        elif i > 1:
            packed, weights, chunks[i - 2], *ends = lax.optimization_barrier((packed, weights, chunks[i - 2], *ends))
        if ends:
            exchanged[k] = ends
        chunks.append(lax.ppermute(packed, "seg", back))
        if 1 <= i <= STEPS:
            edges = [chunks[i - 1][0]] + ([sensor_edges[i - 1][:, None]] if i < STEPS else [])
            exchanged.append(swapped(edges, (0, 1) if i < STEPS else (1,)))
    halos = sum(exchanged, [])
    for number in range(ran, len(stages)):
        run(number)
    return out


def solution(mesh):
    in_specs = (P("seg", None, "gx", None, None), P("seg", "gx", None, None), P(), P())
    out_specs = P("seg", None, "gx", None, None)
    return jax.shard_map(shards, mesh=mesh, in_specs=in_specs, out_specs=out_specs, check_vma=False)
```
